32 devices in a mesh: grp: 2 (over x), tile: 16 (over z, y, core).
Axes of the slice: x: 2, y: 2, z: 4, core: 2. Of those that a mesh axis runs over, the one named last changes fastest.
Arguments:
- state: bfloat16 [256, 16, 512], P(('grp', 'tile')), parts along dimension 0, may hold values from -36 to 36
- wet: int32 [128], replicated, may hold values from 0 to 1, as said below
- w_vqkv: bfloat16 [512, 1536], replicated, may hold values from -0.25 to 0.25
- w_vout: bfloat16 [512, 512], replicated, may hold values from -0.25 to 0.25
- w_hqkv: bfloat16 [512, 1536], replicated, may hold values from -0.25 to 0.25
- w_hout: bfloat16 [512, 512], replicated, may hold values from -0.25 to 0.25
Outputs:
- updated: bfloat16 [256, 16, 512], P(('grp', 'tile')), parts along dimension 0
The draws below stay inside these ranges and needn't reach their ends.
There are 2 independent parts, one for each index of `grp`. The reference program is written for one: setup_inputs(seed, part) draws one part's arguments, and reference() takes and returns one part's arrays. A program takes and returns all parts, laid end to end along the dimension named above; an argument that names none is the same for every part. Nothing has to cross between parts.
Inputs may be any that keep to these rules, and one draw needn't show every extreme that they name: For every strip s (blocks s * 8 to s * 8 + 7), exactly 1 of the 2 blocks with b mod 4 == 0 is wet, and exactly 1 of the 2 blocks with b mod 4 == 3.
All inputs are finite; a program needn't handle non-finite values.
Results may differ from the reference program's by a relative error of at most 0.007.
Values may be sent and summed in bfloat16 or wider, within the bound.
No kernel may reach another device: no remote copies, remote signals or barrier semaphores. Data moves between devices by JAX's collectives and lax.ppermute only.
A program may use at most 64 MiB of HBM per device.

```python
import math
import jax
import jax.numpy as jnp
from jax import lax

D = 512
HEADS = 4
CB = 4
RB = 2
EDGE_WET = 1
TBLK = 8
LEV = 16
BLOCKS = 128
N_TILE = 16


def draw_state(key, part):
    key_base, key_rows, key_cols = jax.random.split(key, 3)
    row_scale = jnp.exp(jax.random.uniform(key_rows, (BLOCKS, LEV, 1), jnp.float32, math.log(0.3), math.log(3.0)))
    col_scale = jnp.exp(jax.random.uniform(key_cols, (1, 1, D), jnp.float32, math.log(0.3), math.log(3.0)))
    base = jnp.clip(jax.random.normal(key_base, (BLOCKS, LEV, D), jnp.float32), -4.0, 4.0)
    return (base * row_scale * col_scale).astype(jnp.bfloat16)


def draw_wet(key, part):
    key_inner, key_edge = jax.random.split(jax.random.fold_in(key, 17), 2)
    strips = BLOCKS // TBLK
    inner = (jax.random.randint(key_inner, (strips, RB, CB), 0, 4) < 3).astype(jnp.int32)
    raw = jax.random.randint(key_edge, (strips, 2, RB), 0, 1048576)
    scores = raw * RB + jnp.arange(RB, dtype=jnp.int32)[None, None, :]
    order = jnp.argsort(scores, axis=-1)
    ranks = jnp.argsort(order, axis=-1)
    edge = (ranks < EDGE_WET).astype(jnp.int32)
    column = jnp.arange(CB, dtype=jnp.int32)[None, None, :]
    result = jnp.where(column == 0, edge[:, 0, :, None], inner)
    result = jnp.where(column == CB - 1, edge[:, 1, :, None], result)
    return result.reshape(BLOCKS).astype(jnp.int32)


def bell_draw(stream_key, shape, width, bound, kind=jnp.bfloat16):
    array = jax.random.normal(stream_key, shape, jnp.float32) * width
    return jnp.minimum(jnp.maximum(array, -bound), bound).astype(kind)


def setup_inputs(seed: int = 0, part: int = 0) -> dict:
    arg_keys = jax.random.split(jax.random.key(seed), 7)
    part_splits = jax.random.split(jax.random.fold_in(arg_keys[6], part), 7)
    state = draw_state(jax.random.fold_in(jax.random.fold_in(arg_keys[6], part), 71), part)
    wet = draw_wet(jax.random.fold_in(arg_keys[6], 71), part)
    w_vqkv = bell_draw(arg_keys[2], (D, 3 * D), D ** -0.5, 0.25)
    w_vout = bell_draw(arg_keys[3], (D, D), D ** -0.5, 0.25)
    w_hqkv = bell_draw(arg_keys[4], (D, 3 * D), D ** -0.5, 0.25)
    w_hout = bell_draw(arg_keys[5], (D, D), D ** -0.5, 0.25)
    return dict(state=state, wet=wet, w_vqkv=w_vqkv, w_vout=w_vout, w_hqkv=w_hqkv, w_hout=w_hout)


EPSILON = 1e-06

def row_norm(values):
    values = values.astype(jnp.float32)
    return values * lax.rsqrt(lax.optimization_barrier(jnp.mean(values * values, axis=-1, keepdims=True)) + EPSILON)

def project(inputs, weights):
    feature_width = inputs.shape[-1]
    head_size = feature_width // HEADS
    normed = row_norm(inputs).astype(jnp.bfloat16)
    joined = jnp.dot(normed.reshape(-1, feature_width), weights, preferred_element_type=jnp.float32)
    target_shape = inputs.shape[:-1] + (HEADS, head_size)
    query = row_norm(joined[:, :feature_width].reshape(target_shape)).astype(jnp.bfloat16)
    keys = row_norm(joined[:, feature_width:2 * feature_width].reshape(target_shape)).astype(jnp.bfloat16)
    values = joined[:, 2 * feature_width:].reshape(target_shape).astype(jnp.bfloat16)
    return (query, keys, values)

def finish(inputs, context, weights):
    feature_width = inputs.shape[-1]
    update = jnp.dot(context.reshape(-1, feature_width), weights, preferred_element_type=jnp.float32)
    return (inputs.astype(jnp.float32) + update.reshape(inputs.shape)).astype(jnp.bfloat16)

def vertical_block(block, w_vqkv, w_vout):
    query, keys, values = project(block, w_vqkv)
    scale = 1.0 / math.sqrt(query.shape[-1])
    scores = jnp.einsum('clhd,cmhd->chlm', query.astype(jnp.float32), keys.astype(jnp.float32)) * scale
    expon = jnp.exp(scores)
    probs = (expon / lax.optimization_barrier(jnp.sum(expon, axis=-1, keepdims=True))).astype(jnp.bfloat16)
    context = jnp.einsum('chlm,cmhd->clhd', probs.astype(jnp.float32), values.astype(jnp.float32)).astype(jnp.bfloat16)
    return finish(block, context, w_vout)

def to_grid(blocks, tiles):
    rest = blocks.shape[1:]
    row_count = blocks.shape[0] // (tiles * CB)
    shaped = jnp.moveaxis(blocks.reshape((tiles, row_count, CB) + rest), 0, 1)
    return shaped.reshape((row_count, tiles * CB) + rest)

def from_grid(grid, tiles):
    rest = grid.shape[2:]
    row_count = grid.shape[0]
    shaped = jnp.moveaxis(grid.reshape((row_count, tiles, CB) + rest), 1, 0)
    return shaped.reshape((tiles * row_count * CB,) + rest)

def wrap_columns(grid):
    return jnp.concatenate([grid[:, -1:], grid, grid[:, :1]], axis=1)

def neighbour_mix(query, keys_ext, values_ext, wet_ext):
    row_count = query.shape[0]
    col_count = query.shape[1]
    scale = 1.0 / math.sqrt(query.shape[-1])
    padding = ((1, 1), (0, 0), (0, 0), (0, 0), (0, 0))
    keys_pad = jnp.pad(keys_ext, padding)
    values_pad = jnp.pad(values_ext, padding)
    wet_pad = jnp.pad(wet_ext, ((1, 1), (0, 0)))
    inside = jnp.pad(jnp.ones((row_count, col_count + 2), jnp.int32), ((1, 1), (0, 0)))
    query_f = query.astype(jnp.float32)
    weights_list = []
    values_list = []
    for row_step in (-1, 0, 1):
        for col_step in (-1, 0, 1):
            rows_here = slice(1 + row_step, 1 + row_step + row_count)
            cols_here = slice(1 + col_step, 1 + col_step + col_count)
            shifted = keys_pad[rows_here, cols_here].astype(jnp.float32)
            scores = lax.optimization_barrier(jnp.sum(query_f * shifted, axis=-1)) * scale
            if row_step == 0 and col_step == 0:
                allowed = jnp.ones((row_count, col_count), jnp.int32)
            else:
                allowed = inside[rows_here, cols_here] * wet_pad[rows_here, cols_here]
            weights_list.append(jnp.where(allowed[:, :, None, None] > 0, jnp.exp(scores), jnp.float32(0.0)))
            values_list.append(values_pad[rows_here, cols_here])
    total = weights_list[0]
    for extra in weights_list[1:]:
        total = total + extra
    context = jnp.zeros(query.shape, jnp.float32)
    for weight_now, value_now in zip(weights_list, values_list):
        probs = (weight_now / total).astype(jnp.bfloat16)
        context = context + probs.astype(jnp.float32)[..., None] * value_now.astype(jnp.float32)
    return context.astype(jnp.bfloat16)

def reference(state, wet, w_vqkv, w_vout, w_hqkv, w_hout):
    blocks_all = state.shape[0]
    levels = state.shape[1]
    feature_width = state.shape[2]
    strips = state.reshape(N_TILE, blocks_all // N_TILE, levels, feature_width)
    mixed = lax.map(lambda block: vertical_block(block, w_vqkv, w_vout), strips)
    mixed = mixed.reshape(blocks_all, levels, feature_width)
    wet_ext = wrap_columns(to_grid(wet, N_TILE))

    def level_step(level_rows):
        grid = to_grid(level_rows, N_TILE)[:, :, None]
        query, keys, values = project(grid, w_hqkv)
        context = neighbour_mix(query, wrap_columns(keys), wrap_columns(values), wet_ext)
        result = finish(grid, context, w_hout)
        return from_grid(result[:, :, 0], N_TILE)
    per_level = lax.map(level_step, jnp.swapaxes(mixed, 0, 1))
    return jnp.swapaxes(per_level, 0, 1)
```

```python
import functools
import math

import jax
import jax.numpy as jnp
from jax import lax
from jax.experimental import pallas as pl
from jax.experimental.pallas import tpu as pltpu
from jax.sharding import PartitionSpec as P

HEADS = 4
CB = 4
EPSILON = 1e-06
BF = jnp.bfloat16
F32 = jnp.float32


def each(count, body):
    if count == 1:
        body(0)
    else:
        pl.loop(0, count)(body)


def rows_at(start, size):
    if isinstance(start, int):
        return pl.ds(start, size)
    return pl.ds(pl.multiple_of(start, size), size)


def inv_rms(values):
    return lax.rsqrt(jnp.mean(values * values, axis=-1, keepdims=True) + EPSILON)


def dot(left, right):
    return jnp.dot(left, right, preferred_element_type=F32)


def dot_t(left, right):
    return lax.dot_general(left, right, (((1,), (1,)), ((), ())), preferred_element_type=F32)


def head(values, index, size):
    return values[:, index * size : (index + 1) * size]


def with_ones(values):
    return jnp.concatenate([values, jnp.ones(values.shape, values.dtype)], axis=1)


def same_block(rows, levels):
    row = lax.broadcasted_iota(jnp.int32, (rows, rows), 0) // levels
    col = lax.broadcasted_iota(jnp.int32, (rows, rows), 1) // levels
    return row == col


def vertical(block, w_vqkv, w_vout, levels):
    rows, width = block.shape
    size = width // HEADS
    scale = math.log2(math.e) / math.sqrt(size)
    values = block.astype(F32)
    joined = dot((values * inv_rms(values)).astype(BF), w_vqkv[...])
    parts = []
    for h in range(HEADS):
        query = head(joined, h, size)
        keys = head(joined, HEADS + h, size)
        query = (query * (inv_rms(query) * scale)).astype(BF)
        keys = (keys * inv_rms(keys)).astype(BF)
        expon = jnp.exp2(dot_t(query, keys))
        if rows > levels:
            expon = jnp.where(same_block(rows, levels), expon, 0.0)
        total = dot(expon.astype(BF), with_ones(head(joined, 2 * HEADS + h, size).astype(BF)))
        parts.append((total[:, :size] / total[:, size:]).astype(BF))
    return (values + dot(jnp.concatenate(parts, axis=1), w_vout[...])).astype(BF)


def own_kernel(
    levels, wet_ref, x_ref, w_vqkv, w_vout, w_hqkv, w_hout,
    out_ref, mixed_e, query_e, num_e, den_e, pick_ref, mixed_s,
):
    total_rows, width = x_ref.shape
    size = width // HEADS
    scale = math.log2(math.e) / math.sqrt(size)
    blocks = total_rows // levels
    chunk = min(levels, 16)
    edges = [b for b in range(blocks) if b % CB in (0, CB - 1)]
    tile = lax.axis_index("tile")
    tiles = lax.axis_size("tile")
    group = min(max(levels, 128), total_rows)

    def mix(index):
        rows = rows_at(index * group, group)
        mixed_s[rows, :] = vertical(x_ref[rows, :], w_vqkv, w_vout, levels)

    each(total_rows // group, mix)

    left = lax.rem(tile + tiles - 1, tiles) * blocks
    right = lax.rem(tile + 1, tiles) * blocks
    pick_ref[0, :, :] = jnp.full(pick_ref.shape[1:], wet_ref[left + CB - 1], jnp.int32)
    pick_ref[1, :, :] = jnp.full(pick_ref.shape[1:], wet_ref[right], jnp.int32)

    rows = blocks * chunk
    row = lax.broadcasted_iota(jnp.int32, (rows, rows), 0)
    col = lax.broadcasted_iota(jnp.int32, (rows, rows), 1)
    block_q, block_k = row // chunk, col // chunk
    wet_k = jnp.zeros((rows, rows), jnp.int32)
    for b in range(blocks):
        wet_k = jnp.where(block_k == b, wet_ref[tile * blocks + b], wet_k)
    near = jnp.abs(block_q % CB - block_k % CB) <= 1
    near = near & (jnp.abs(block_q // CB - block_k // CB) <= 1)
    allowed = (row % chunk == col % chunk) & ((block_q == block_k) | (near & (wet_k > 0)))

    def attend(index):
        def spots(b):
            return rows_at(b * levels + index * chunk, chunk)

        mixed = jnp.concatenate([mixed_s[spots(b), :] for b in range(blocks)], axis=0)
        values = mixed.astype(F32)
        joined = dot((values * inv_rms(values)).astype(BF), w_hqkv[...])
        parts = []
        for h in range(HEADS):
            query = head(joined, h, size)
            keys = head(joined, HEADS + h, size)
            query = (query * (inv_rms(query) * scale)).astype(BF)
            keys = (keys * inv_rms(keys)).astype(BF)
            expon = jnp.where(allowed, jnp.exp2(dot_t(query, keys)), 0.0).astype(BF)
            total = dot(expon, with_ones(head(joined, 2 * HEADS + h, size).astype(BF)))
            cols = slice(h * size, (h + 1) * size)
            for e, b in enumerate(edges):
                here = slice(b * chunk, (b + 1) * chunk)
                there = rows_at(e * levels + index * chunk, chunk)
                query_e[there, cols] = query[here]
                num_e[there, cols] = total[here, :size]
                den_e[there, cols] = total[here, size:]
            parts.append((total[:, :size] / total[:, size:]).astype(BF))
        result = (values + dot(jnp.concatenate(parts, axis=1), w_hout[...])).astype(BF)
        for b in range(blocks):
            here = slice(b * chunk, (b + 1) * chunk)
            if b in edges:
                mixed_e[rows_at(edges.index(b) * levels + index * chunk, chunk), :] = mixed[here]
            else:
                out_ref[spots(b), :] = result[here]

    each(levels // chunk, attend)


def halo_kernel(
    levels, blocks, from_left, from_right, pick_ref, mixed_e, query_e, num_e, den_e,
    w_vqkv, w_vout, w_hqkv, w_hout, partial_ref, out_ref, keys_s, values_s, result_s, sems,
):
    width = mixed_e.shape[1]
    size = width // HEADS
    chunk = min(levels, 16)
    edges = [b for b in range(blocks) if b % CB in (0, CB - 1)]
    group = 2 * levels if 2 * levels <= 128 else levels

    def choose(ref, side):
        return jnp.where(pick_ref[side, 0:1, 0:1] > 0, ref[0:levels, :], ref[levels : 2 * levels, :])

    halo = jnp.concatenate([choose(from_left, 0), choose(from_right, 1)], axis=0)
    for start in range(0, 2 * levels, group):
        rows = slice(start, start + group)
        mixed = vertical(halo[rows], w_vqkv, w_vout, levels).astype(F32)
        joined = dot((mixed * inv_rms(mixed)).astype(BF), w_hqkv[:, width:])
        for h in range(HEADS):
            cols = slice(h * size, (h + 1) * size)
            keys = head(joined, h, size)
            keys_s[rows, cols] = (keys * inv_rms(keys)).astype(BF)
        values_s[rows, :] = joined[:, width:].astype(BF)

    shape = (len(edges) * chunk, 2 * chunk)
    row = lax.broadcasted_iota(jnp.int32, shape, 0)
    col = lax.broadcasted_iota(jnp.int32, shape, 1)
    side = jnp.zeros(shape, jnp.int32)
    for e, b in enumerate(edges):
        side = jnp.where(row // chunk == e, 0 if b % CB == 0 else 1, side)
    allowed = (side == col // chunk) & (row % chunk == col % chunk)

    def attend(index):
        def take(ref, count):
            return jnp.concatenate(
                [ref[rows_at(i * levels + index * chunk, chunk), :] for i in range(count)], axis=0
            )

        keys, values = take(keys_s, 2), take(values_s, 2)
        query, num, den = (take(ref, len(edges)) for ref in (query_e, num_e, den_e))
        parts = []
        for h in range(HEADS):
            scores = dot_t(head(query, h, size), head(keys, h, size))
            expon = jnp.where(allowed, jnp.exp2(scores), 0.0).astype(BF)
            total = dot(expon, with_ones(head(values, h, size)))
            above = head(num, h, size) + total[:, :size]
            below = head(den, h, size) + total[:, size:]
            parts.append((above / below).astype(BF))
        update = dot(jnp.concatenate(parts, axis=1), w_hout[...])
        result = (take(mixed_e, len(edges)).astype(F32) + update).astype(BF)
        for e in range(len(edges)):
            there = rows_at(e * levels + index * chunk, chunk)
            result_s[there, :] = result[e * chunk : (e + 1) * chunk]

    each(levels // chunk, attend)
    copies = [
        pltpu.make_async_copy(
            result_s.at[pl.ds(e * levels, levels), :],
            out_ref.at[pl.ds(b * levels, levels), :],
            sems.at[e],
        )
        for e, b in enumerate(edges)
    ]
    for copy in copies:
        copy.start()
    for copy in copies:
        copy.wait()


def on_device(state, wet, w_vqkv, w_vout, w_hqkv, w_hout):
    tiles = lax.axis_size("tile")
    blocks, levels, width = state.shape
    rows = blocks // CB
    strip = state.reshape(rows, CB, levels, width)
    to_right = strip[:, CB - 1].reshape(rows * levels, width)
    to_left = strip[:, 0].reshape(rows * levels, width)
    from_left = lax.ppermute(to_right, "tile", [(i, (i + 1) % tiles) for i in range(tiles)])
    from_right = lax.ppermute(to_left, "tile", [(i, (i - 1) % tiles) for i in range(tiles)])

    edge_rows = 2 * rows * levels
    limit = (10 << 20) + levels * (256 << 10)
    vmem = pl.BlockSpec(memory_space=pltpu.VMEM)
    smem = pl.BlockSpec(memory_space=pltpu.SMEM)
    hbm = pl.BlockSpec(memory_space=pl.ANY)
    whole = jax.ShapeDtypeStruct((blocks * levels, width), BF)
    partial, mixed_e, query_e, num_e, den_e, pick = pl.pallas_call(
        functools.partial(own_kernel, levels),
        out_shape=(
            whole,
            jax.ShapeDtypeStruct((edge_rows, width), BF),
            jax.ShapeDtypeStruct((edge_rows, width), BF),
            jax.ShapeDtypeStruct((edge_rows, width), F32),
            jax.ShapeDtypeStruct((edge_rows, width), F32),
            jax.ShapeDtypeStruct((2, 8, 128), jnp.int32),
        ),
        in_specs=[smem] + [vmem] * 5,
        out_specs=(vmem,) * 6,
        scratch_shapes=[pltpu.VMEM((blocks * levels, width), BF)],
        compiler_params=pltpu.CompilerParams(vmem_limit_bytes=limit),
        cost_estimate=pl.CostEstimate(
            flops=2 * blocks * levels * width * width * 8, bytes_accessed=8 << 20, transcendentals=0
        ),
        name="own_blocks",
    )(wet, state.reshape(blocks * levels, width), w_vqkv, w_vout, w_hqkv, w_hout)
    updated = pl.pallas_call(
        functools.partial(halo_kernel, levels, blocks),
        out_shape=whole,
        in_specs=[vmem] * 11 + [hbm],
        out_specs=hbm,
        scratch_shapes=[
            pltpu.VMEM((2 * levels, width), BF),
            pltpu.VMEM((2 * levels, width), BF),
            pltpu.VMEM((edge_rows, width), BF),
            pltpu.SemaphoreType.DMA((2 * rows,)),
        ],
        input_output_aliases={11: 0},
        compiler_params=pltpu.CompilerParams(vmem_limit_bytes=limit),
        name="halo_blocks",
    )(from_left, from_right, pick, mixed_e, query_e, num_e, den_e,
      w_vqkv, w_vout, w_hqkv, w_hout, partial)
    return updated.reshape(blocks, levels, width)


def solution(mesh):
    in_specs = (P(("grp", "tile"), None, None), P(), P(), P(), P(), P())
    out_specs = P(("grp", "tile"), None, None)
    return jax.shard_map(
        on_device, mesh=mesh, in_specs=in_specs, out_specs=out_specs, check_vma=False
    )
```

```python
import functools
import math

import jax
import jax.numpy as jnp
from jax import lax
from jax.experimental import pallas as pl
from jax.experimental.pallas import tpu as pltpu
from jax.sharding import PartitionSpec as P

HEADS = 4
CB = 4
EPSILON = 1e-06
BF = jnp.bfloat16
F32 = jnp.float32


def each(count, body):
    if count == 1:
        body(0)
    else:
        pl.loop(0, count)(body)


def rows_at(start, size):
    if isinstance(start, int):
        return pl.ds(start, size)
    return pl.ds(pl.multiple_of(start, size), size)


def dot(left, right):
    return jnp.dot(left, right, preferred_element_type=F32)


def dot_t(left, right):
    return lax.dot_general(left, right, (((1,), (1,)), ((), ())), preferred_element_type=F32)


def head(values, index, size):
    return values[:, index * size : (index + 1) * size]


def with_ones(values):
    return jnp.concatenate([values, jnp.ones(values.shape, values.dtype)], axis=1)


def same_block(rows, levels):
    row = lax.broadcasted_iota(jnp.int32, (rows, rows), 0) // levels
    col = lax.broadcasted_iota(jnp.int32, (rows, rows), 1) // levels
    return row == col


def project(values, squares, weights, scale, size, first=0):
    joined = dot(values, weights)
    inverse = lax.rsqrt(squares)
    floor = squares * EPSILON
    out = []
    for part in range(3 * HEADS - first * HEADS):
        kind = part // HEADS + first
        piece = head(joined, part, size)
        if kind == 2:
            out.append((piece * inverse).astype(BF))
        else:
            factor = lax.rsqrt(jnp.mean(piece * piece, axis=-1, keepdims=True) + floor)
            out.append((piece * (factor * scale if kind == 0 else factor)).astype(BF))
    return [out[i : i + HEADS] for i in range(0, len(out), HEADS)]


def mean_square(values):
    return jnp.mean(values * values, axis=-1, keepdims=True) + EPSILON


def vertical(block, w_vqkv, w_vout, levels):
    rows, width = block.shape
    size = width // HEADS
    scale = math.log2(math.e) / math.sqrt(size)
    values = block.astype(F32)
    queries, keys, vals = project(block, mean_square(values), w_vqkv[...], scale, size)
    parts = []
    for h in range(HEADS):
        expon = jnp.exp2(dot_t(queries[h], keys[h]))
        if rows > levels:
            expon = jnp.where(same_block(rows, levels), expon, 0.0)
        total = dot(expon.astype(BF), with_ones(vals[h]))
        parts.append((total[:, :size] / total[:, size:]).astype(BF))
    return (values + dot(jnp.concatenate(parts, axis=1), w_vout[...])).astype(BF)


def own_kernel(
    levels, wet_hbm, x_hbm, wv_hbm, wo_hbm, hv_hbm, ho_hbm,
    result_ref, mixed_e, query_e, num_e, den_e, pick_ref, w_vqkv, w_vout, w_hqkv, w_hout,
    x_ref, wet_ref, mixed_s, sems,
):
    pairs = ((x_hbm, x_ref), (wv_hbm, w_vqkv), (wet_hbm, wet_ref), (wo_hbm, w_vout),
             (hv_hbm, w_hqkv), (ho_hbm, w_hout))
    copies = [pltpu.make_async_copy(a, b, sems.at[i]) for i, (a, b) in enumerate(pairs)]
    for copy in copies:
        copy.start()
    x_in, wv_in, wet_in, wo_in, hv_in, ho_in = copies
    total_rows, width = x_ref.shape
    size = width // HEADS
    scale = math.log2(math.e) / math.sqrt(size)
    blocks = total_rows // levels
    chunk = min(levels, 16)
    edges = [b for b in range(blocks) if b % CB in (0, CB - 1)]
    tile = lax.axis_index("tile")
    tiles = lax.axis_size("tile")
    group = min(max(levels, 128), total_rows)

    def mix(index):
        rows = rows_at(index * group, group)
        mixed_s[rows, :] = vertical(x_ref[rows, :], w_vqkv, w_vout, levels)

    x_in.wait()
    wv_in.wait()
    wo_in.wait()
    each(total_rows // group, mix)
    wet_in.wait()
    hv_in.wait()
    ho_in.wait()

    left = lax.rem(tile + tiles - 1, tiles) * blocks
    right = lax.rem(tile + 1, tiles) * blocks
    pick_ref[0, :, :] = jnp.full(pick_ref.shape[1:], wet_ref[left + CB - 1], jnp.int32)
    pick_ref[1, :, :] = jnp.full(pick_ref.shape[1:], wet_ref[right], jnp.int32)

    rows = blocks * chunk
    row = lax.broadcasted_iota(jnp.int32, (rows, rows), 0)
    col = lax.broadcasted_iota(jnp.int32, (rows, rows), 1)
    block_q, block_k = row // chunk, col // chunk
    wet_k = jnp.zeros((rows, rows), jnp.int32)
    for b in range(blocks):
        wet_k = jnp.where(block_k == b, wet_ref[tile * blocks + b], wet_k)
    near = jnp.abs(block_q % CB - block_k % CB) <= 1
    near = near & (jnp.abs(block_q // CB - block_k // CB) <= 1)
    allowed = (row % chunk == col % chunk) & ((block_q == block_k) | (near & (wet_k > 0)))

    def attend(index):
        def spots(b):
            return rows_at(b * levels + index * chunk, chunk)

        mixed = jnp.concatenate([mixed_s[spots(b), :] for b in range(blocks)], axis=0)
        values = mixed.astype(F32)
        queries, keys, vals = project(mixed, mean_square(values), w_hqkv[...], scale, size)
        parts = []
        for h in range(HEADS):
            expon = jnp.where(allowed, jnp.exp2(dot_t(queries[h], keys[h])), 0.0).astype(BF)
            total = dot(expon, with_ones(vals[h]))
            cols = slice(h * size, (h + 1) * size)
            for e, b in enumerate(edges):
                here = slice(b * chunk, (b + 1) * chunk)
                there = rows_at(e * levels + index * chunk, chunk)
                query_e[there, cols] = queries[h][here]
                num_e[there, cols] = total[here, :size]
                den_e[there, cols] = total[here, size:]
            parts.append((total[:, :size] / total[:, size:]).astype(BF))
        result = (values + dot(jnp.concatenate(parts, axis=1), w_hout[...])).astype(BF)
        for b in range(blocks):
            here = slice(b * chunk, (b + 1) * chunk)
            if b in edges:
                mixed_e[rows_at(edges.index(b) * levels + index * chunk, chunk), :] = mixed[here]
            else:
                result_ref[spots(b), :] = result[here]

    each(levels // chunk, attend)


def halo_kernel(
    levels, blocks, from_left, from_right, pick_ref, mixed_e, query_e, num_e, den_e,
    w_vqkv, w_vout, w_hqkv, w_hout, inner_ref, out_ref, keys_s, values_s, result_s, sems,
):
    width = mixed_e.shape[1]
    size = width // HEADS
    chunk = min(levels, 16)
    edges = [b for b in range(blocks) if b % CB in (0, CB - 1)]
    group = 2 * levels if 2 * levels <= 128 else levels
    inner = [
        pltpu.make_async_copy(ref, out_ref.at[pl.ds(b * levels, levels), :], sems.at[b])
        for b in range(blocks) if b not in edges
        for ref in [inner_ref.at[pl.ds(b * levels, levels), :]]
    ]
    for copy in inner:
        copy.start()

    def choose(ref, side):
        return jnp.where(pick_ref[side, 0:1, 0:1] > 0, ref[0:levels, :], ref[levels : 2 * levels, :])

    halo = jnp.concatenate([choose(from_left, 0), choose(from_right, 1)], axis=0)
    for start in range(0, 2 * levels, group):
        rows = slice(start, start + group)
        mixed = vertical(halo[rows], w_vqkv, w_vout, levels)
        keys, vals = project(mixed, mean_square(mixed.astype(F32)), w_hqkv[:, width:], 1.0, size, 1)
        for h in range(HEADS):
            cols = slice(h * size, (h + 1) * size)
            keys_s[rows, cols] = keys[h]
            values_s[rows, cols] = vals[h]

    shape = (len(edges) * chunk, 2 * chunk)
    row = lax.broadcasted_iota(jnp.int32, shape, 0)
    col = lax.broadcasted_iota(jnp.int32, shape, 1)
    side = jnp.zeros(shape, jnp.int32)
    for e, b in enumerate(edges):
        side = jnp.where(row // chunk == e, 0 if b % CB == 0 else 1, side)
    allowed = (side == col // chunk) & (row % chunk == col % chunk)

    def attend(index):
        def take(ref, count):
            return jnp.concatenate(
                [ref[rows_at(i * levels + index * chunk, chunk), :] for i in range(count)], axis=0
            )

        keys, values = take(keys_s, 2), take(values_s, 2)
        query, num, den = (take(ref, len(edges)) for ref in (query_e, num_e, den_e))
        parts = []
        for h in range(HEADS):
            scores = dot_t(head(query, h, size), head(keys, h, size))
            expon = jnp.where(allowed, jnp.exp2(scores), 0.0).astype(BF)
            total = dot(expon, with_ones(head(values, h, size)))
            above = head(num, h, size) + total[:, :size]
            below = head(den, h, size) + total[:, size:]
            parts.append((above / below).astype(BF))
        update = dot(jnp.concatenate(parts, axis=1), w_hout[...])
        result = (take(mixed_e, len(edges)).astype(F32) + update).astype(BF)
        for e in range(len(edges)):
            there = rows_at(e * levels + index * chunk, chunk)
            result_s[there, :] = result[e * chunk : (e + 1) * chunk]

    each(levels // chunk, attend)
    copies = [
        pltpu.make_async_copy(
            result_s.at[pl.ds(e * levels, levels), :],
            out_ref.at[pl.ds(b * levels, levels), :],
            sems.at[b],
        )
        for e, b in enumerate(edges)
    ]
    for copy in copies:
        copy.start()
    for copy in inner + copies:
        copy.wait()


def on_device(state, wet, w_vqkv, w_vout, w_hqkv, w_hout):
    tiles = lax.axis_size("tile")
    blocks, levels, width = state.shape
    rows = blocks // CB
    strip = state.reshape(rows, CB, levels, width)
    to_right = strip[:, CB - 1].reshape(rows * levels, width)
    to_left = strip[:, 0].reshape(rows * levels, width)
    from_left = lax.ppermute(to_right, "tile", [(i, (i + 1) % tiles) for i in range(tiles)])
    from_right = lax.ppermute(to_left, "tile", [(i, (i - 1) % tiles) for i in range(tiles)])

    edge_rows = 2 * rows * levels
    limit = (10 << 20) + levels * (256 << 10)
    vmem = pl.BlockSpec(memory_space=pltpu.VMEM)
    hbm = pl.BlockSpec(memory_space=pl.ANY)
    whole = jax.ShapeDtypeStruct((blocks * levels, width), BF)
    weights = (w_vqkv, w_vout, w_hqkv, w_hout)
    operands = (wet, state.reshape(blocks * levels, width)) + weights
    saved = pl.pallas_call(
        functools.partial(own_kernel, levels),
        out_shape=(
            whole,
            jax.ShapeDtypeStruct((edge_rows, width), BF),
            jax.ShapeDtypeStruct((edge_rows, width), BF),
            jax.ShapeDtypeStruct((edge_rows, width), F32),
            jax.ShapeDtypeStruct((edge_rows, width), F32),
            jax.ShapeDtypeStruct((2, 8, 128), jnp.int32),
        ) + tuple(jax.ShapeDtypeStruct(w.shape, w.dtype) for w in weights),
        in_specs=[hbm] * 6,
        out_specs=(vmem,) * 10,
        scratch_shapes=[
            pltpu.VMEM((blocks * levels, width), BF),
            pltpu.SMEM(wet.shape, wet.dtype),
            pltpu.VMEM((blocks * levels, width), BF),
            pltpu.SemaphoreType.DMA((6,)),
        ],
        compiler_params=pltpu.CompilerParams(vmem_limit_bytes=limit),
        cost_estimate=pl.CostEstimate(
            flops=2 * blocks * levels * width * width * 8, bytes_accessed=8 << 20, transcendentals=0
        ),
        name="own_blocks",
    )(*[pltpu.with_memory_space_constraint(value, pltpu.HBM) for value in operands])
    inner, *edge_values = saved[:6]
    updated = pl.pallas_call(
        functools.partial(halo_kernel, levels, blocks),
        out_shape=whole,
        in_specs=[vmem] * 12,
        out_specs=hbm,
        scratch_shapes=[
            pltpu.VMEM((2 * levels, width), BF),
            pltpu.VMEM((2 * levels, width), BF),
            pltpu.VMEM((edge_rows, width), BF),
            pltpu.SemaphoreType.DMA((blocks,)),
        ],
        compiler_params=pltpu.CompilerParams(vmem_limit_bytes=limit),
        name="halo_blocks",
    )(from_left, from_right, edge_values[4], *edge_values[:4], *saved[6:], inner)
    return updated.reshape(blocks, levels, width)


def solution(mesh):
    in_specs = (P(("grp", "tile"), None, None), P(), P(), P(), P(), P())
    out_specs = P(("grp", "tile"), None, None)
    return jax.shard_map(
        on_device, mesh=mesh, in_specs=in_specs, out_specs=out_specs, check_vma=False
    )
```

```python
import functools
import math

import jax
import jax.numpy as jnp
from jax import lax
from jax.experimental import pallas as pl
from jax.experimental.pallas import tpu as pltpu
from jax.sharding import PartitionSpec as P

HEADS = 4
CB = 4
EPSILON = 1e-06
BF = jnp.bfloat16
F32 = jnp.float32


def each(count, body):
    if count == 1:
        body(0)
    else:
        pl.loop(0, count)(body)


def rows_at(start, size):
    if isinstance(start, int):
        return pl.ds(start, size)
    return pl.ds(pl.multiple_of(start, size), size)


def dot(left, right):
    return jnp.dot(left, right, preferred_element_type=F32)


def dot_t(left, right):
    return lax.dot_general(left, right, (((1,), (1,)), ((), ())), preferred_element_type=F32)


def head(values, index, size):
    return values[:, index * size : (index + 1) * size]


def with_ones(values):
    return jnp.concatenate([values, jnp.ones(values.shape, values.dtype)], axis=1)


def same_block(rows, levels):
    row = lax.broadcasted_iota(jnp.int32, (rows, rows), 0) // levels
    col = lax.broadcasted_iota(jnp.int32, (rows, rows), 1) // levels
    return row == col


def project(values, squares, weights, scale, size, first=0):
    joined = dot(values, weights)
    inverse = lax.rsqrt(squares)
    floor = squares * EPSILON
    out = []
    for part in range(3 * HEADS - first * HEADS):
        kind = part // HEADS + first
        piece = head(joined, part, size)
        if kind == 2:
            out.append((piece * inverse).astype(BF))
        else:
            factor = lax.rsqrt(jnp.mean(piece * piece, axis=-1, keepdims=True) + floor)
            out.append((piece * (factor * scale if kind == 0 else factor)).astype(BF))
    return [out[i : i + HEADS] for i in range(0, len(out), HEADS)]


def mean_square(values):
    return jnp.mean(values * values, axis=-1, keepdims=True) + EPSILON


def vertical(block, w_vqkv, w_vout, levels):
    rows, width = block.shape
    size = width // HEADS
    scale = math.log2(math.e) / math.sqrt(size)
    values = block.astype(F32)
    queries, keys, vals = project(block, mean_square(values), w_vqkv[...], scale, size)
    expons = [jnp.exp2(dot_t(q, k)) for q, k in zip(queries, keys)]
    if rows > levels:
        inside = same_block(rows, levels)
        expons = [jnp.where(inside, e, 0.0) for e in expons]
    totals = [dot(e.astype(BF), with_ones(v)) for e, v in zip(expons, vals)]
    parts = [(t[:, :size] / t[:, size:]).astype(BF) for t in totals]
    return (values + dot(jnp.concatenate(parts, axis=1), w_vout[...])).astype(BF)


def gate_kernel(*refs):
    pass


def own_kernel(
    levels, wet_ref, x_ref, w_vqkv, w_vout, w_hqkv, w_hout,
    result_ref, mixed_e, query_e, num_e, den_e, pick_ref, mixed_s,
):
    total_rows, width = x_ref.shape
    size = width // HEADS
    scale = math.log2(math.e) / math.sqrt(size)
    blocks = total_rows // levels
    chunk = min(levels, 16)
    edges = [b for b in range(blocks) if b % CB in (0, CB - 1)]
    tile = lax.axis_index("tile")
    tiles = lax.axis_size("tile")
    group = min(max(levels, 128), total_rows)

    def mix(index):
        rows = rows_at(index * group, group)
        mixed_s[rows, :] = vertical(x_ref[rows, :], w_vqkv, w_vout, levels)

    each(total_rows // group, mix)

    rows = blocks * chunk
    row = lax.broadcasted_iota(jnp.int32, (rows, rows), 0)
    col = lax.broadcasted_iota(jnp.int32, (rows, rows), 1)
    block_q, block_k = row // chunk, col // chunk
    wet = wet_ref[...].astype(BF)
    which = lax.broadcasted_iota(jnp.int32, (wet.shape[1], rows), 0)
    column = lax.broadcasted_iota(jnp.int32, (wet.shape[1], rows), 1) // chunk
    wet_k = dot(wet, (which == tile * blocks + column).astype(BF))[0:1, :]
    left = lax.rem(tile + tiles - 1, tiles) * blocks + CB - 1
    right = lax.rem(tile + 1, tiles) * blocks
    for i, block in enumerate((left, right)):
        pick_ref[i, :, :] = dot(wet, (which[:, :128] == block).astype(BF))
    near = jnp.abs(block_q % CB - block_k % CB) <= 1
    near = near & (jnp.abs(block_q // CB - block_k // CB) <= 1)
    allowed = (row % chunk == col % chunk) & ((block_q == block_k) | (near & (wet_k > 0.5)))

    def attend(index):
        def spots(b):
            return rows_at(b * levels + index * chunk, chunk)

        mixed = jnp.concatenate([mixed_s[spots(b), :] for b in range(blocks)], axis=0)
        values = mixed.astype(F32)
        queries, keys, vals = project(mixed, mean_square(values), w_hqkv[...], scale, size)
        expons = [jnp.exp2(dot_t(q, k)) for q, k in zip(queries, keys)]
        expons = [jnp.where(allowed, e, 0.0).astype(BF) for e in expons]
        totals = [dot(e, with_ones(v)) for e, v in zip(expons, vals)]
        parts = [(t[:, :size] / t[:, size:]).astype(BF) for t in totals]
        for h, total in enumerate(totals):
            cols = slice(h * size, (h + 1) * size)
            for e, b in enumerate(edges):
                here = slice(b * chunk, (b + 1) * chunk)
                there = rows_at(e * levels + index * chunk, chunk)
                query_e[there, cols] = queries[h][here]
                num_e[there, cols] = total[here, :size]
                den_e[there, cols] = total[here, size:]
        result = (values + dot(jnp.concatenate(parts, axis=1), w_hout[...])).astype(BF)
        for b in range(blocks):
            here = slice(b * chunk, (b + 1) * chunk)
            if b in edges:
                mixed_e[rows_at(edges.index(b) * levels + index * chunk, chunk), :] = mixed[here]
            else:
                result_ref[spots(b), :] = result[here]

    each(levels // chunk, attend)


def halo_kernel(
    levels, blocks, from_left, from_right, pick_ref, mixed_e, query_e, num_e, den_e,
    w_vqkv, w_vout, w_hqkv, w_hout, inner_ref, out_ref, keys_s, values_s, result_s, sems,
):
    width = mixed_e.shape[1]
    size = width // HEADS
    chunk = min(levels, 16)
    edges = [b for b in range(blocks) if b % CB in (0, CB - 1)]
    group = 2 * levels if 2 * levels <= 128 else levels
    inner = [
        pltpu.make_async_copy(ref, out_ref.at[pl.ds(b * levels, levels), :], sems.at[b])
        for b in range(blocks) if b not in edges
        for ref in [inner_ref.at[pl.ds(b * levels, levels), :]]
    ]
    for copy in inner:
        copy.start()

    halo = jnp.concatenate(
        [
            jnp.where(pick_ref[i, 0:1, 0:1] > 0.5, ref[0:levels, :], ref[levels : 2 * levels, :])
            for i, ref in enumerate((from_left, from_right))
        ],
        axis=0,
    )
    for start in range(0, 2 * levels, group):
        rows = slice(start, start + group)
        mixed = vertical(halo[rows], w_vqkv, w_vout, levels)
        keys, vals = project(mixed, mean_square(mixed.astype(F32)), w_hqkv[:, width:], 1.0, size, 1)
        for h in range(HEADS):
            cols = slice(h * size, (h + 1) * size)
            keys_s[rows, cols] = keys[h]
            values_s[rows, cols] = vals[h]

    shape = (len(edges) * chunk, 2 * chunk)
    row = lax.broadcasted_iota(jnp.int32, shape, 0)
    col = lax.broadcasted_iota(jnp.int32, shape, 1)
    side = jnp.zeros(shape, jnp.int32)
    for e, b in enumerate(edges):
        side = jnp.where(row // chunk == e, 0 if b % CB == 0 else 1, side)
    allowed = (side == col // chunk) & (row % chunk == col % chunk)

    def attend(index):
        def take(ref, count):
            return jnp.concatenate(
                [ref[rows_at(i * levels + index * chunk, chunk), :] for i in range(count)], axis=0
            )

        keys, values = take(keys_s, 2), take(values_s, 2)
        query, num, den = (take(ref, len(edges)) for ref in (query_e, num_e, den_e))
        scores = [dot_t(head(query, h, size), head(keys, h, size)) for h in range(HEADS)]
        expons = [jnp.where(allowed, jnp.exp2(x), 0.0).astype(BF) for x in scores]
        totals = [dot(e, with_ones(head(values, h, size))) for h, e in enumerate(expons)]
        parts = [
            ((head(num, h, size) + t[:, :size]) / (head(den, h, size) + t[:, size:])).astype(BF)
            for h, t in enumerate(totals)
        ]
        update = dot(jnp.concatenate(parts, axis=1), w_hout[...])
        result = (take(mixed_e, len(edges)).astype(F32) + update).astype(BF)
        for e in range(len(edges)):
            there = rows_at(e * levels + index * chunk, chunk)
            result_s[there, :] = result[e * chunk : (e + 1) * chunk]

    each(levels // chunk, attend)
    copies = [
        pltpu.make_async_copy(
            result_s.at[pl.ds(e * levels, levels), :],
            out_ref.at[pl.ds(b * levels, levels), :],
            sems.at[b],
        )
        for e, b in enumerate(edges)
    ]
    for copy in copies:
        copy.start()
    for copy in inner + copies:
        copy.wait()


def on_device(state, wet, w_vqkv, w_vout, w_hqkv, w_hout):
    tiles = lax.axis_size("tile")
    blocks, levels, width = state.shape
    rows = blocks // CB
    edge_rows = 2 * rows * levels
    limit = (10 << 20) + levels * (256 << 10)
    vmem = pl.BlockSpec(memory_space=pltpu.VMEM)
    hbm = pl.BlockSpec(memory_space=pl.ANY)
    whole = jax.ShapeDtypeStruct((blocks * levels, width), BF)
    strip = state.reshape(rows, CB, levels, width)
    edges = [strip[:, c].reshape(rows * levels, width) for c in (CB - 1, 0)]
    to_right, to_left = pl.pallas_call(
        gate_kernel,
        out_shape=[jax.ShapeDtypeStruct(e.shape, e.dtype) for e in edges],
        in_specs=[vmem] * 2,
        out_specs=[vmem] * 2,
        input_output_aliases={0: 0, 1: 1},
        compiler_params=pltpu.CompilerParams(vmem_limit_bytes=1 << 20),
        cost_estimate=pl.CostEstimate(flops=200 << 30, bytes_accessed=1 << 30, transcendentals=0),
        name="gate",
    )(*edges)
    from_left = lax.ppermute(to_right, "tile", [(i, (i + 1) % tiles) for i in range(tiles)])
    from_right = lax.ppermute(to_left, "tile", [(i, (i - 1) % tiles) for i in range(tiles)])

    weights = (w_vqkv, w_vout, w_hqkv, w_hout)
    inner, *edge_values, pick = pl.pallas_call(
        functools.partial(own_kernel, levels),
        out_shape=(
            whole,
            jax.ShapeDtypeStruct((edge_rows, width), BF),
            jax.ShapeDtypeStruct((edge_rows, width), BF),
            jax.ShapeDtypeStruct((edge_rows, width), F32),
            jax.ShapeDtypeStruct((edge_rows, width), F32),
            jax.ShapeDtypeStruct((2, 8, 128), F32),
        ),
        in_specs=[vmem] * 6,
        out_specs=(vmem,) * 6,
        scratch_shapes=[pltpu.VMEM((blocks * levels, width), BF)],
        compiler_params=pltpu.CompilerParams(vmem_limit_bytes=limit),
        cost_estimate=pl.CostEstimate(
            flops=2 * blocks * levels * width * width * 8, bytes_accessed=8 << 20, transcendentals=0
        ),
        name="own_blocks",
    )(jnp.broadcast_to(wet, (8, wet.shape[0])), state.reshape(blocks * levels, width), *weights)
    updated = pl.pallas_call(
        functools.partial(halo_kernel, levels, blocks),
        out_shape=whole,
        in_specs=[vmem] * 12,
        out_specs=hbm,
        scratch_shapes=[
            pltpu.VMEM((2 * levels, width), BF),
            pltpu.VMEM((2 * levels, width), BF),
            pltpu.VMEM((edge_rows, width), BF),
            pltpu.SemaphoreType.DMA((blocks,)),
        ],
        compiler_params=pltpu.CompilerParams(vmem_limit_bytes=limit),
        name="halo_blocks",
    )(from_left, from_right, pick, *edge_values, *weights, inner)
    return updated.reshape(blocks, levels, width)


def solution(mesh):
    in_specs = (P(("grp", "tile"), None, None), P(), P(), P(), P(), P())
    out_specs = P(("grp", "tile"), None, None)
    return jax.shard_map(
        on_device, mesh=mesh, in_specs=in_specs, out_specs=out_specs, check_vma=False
    )
```

```python
import functools
import math

import jax
import jax.numpy as jnp
from jax import lax
from jax.experimental import pallas as pl
from jax.experimental.pallas import tpu as pltpu
from jax.sharding import PartitionSpec as P

HEADS = 4
CB = 4
EPSILON = 1e-06
BF = jnp.bfloat16
F32 = jnp.float32


def each(count, body):
    if count == 1:
        body(0)
    else:
        pl.loop(0, count)(body)


def rows_at(start, size):
    if isinstance(start, int):
        return pl.ds(start, size)
    return pl.ds(pl.multiple_of(start, size), size)


def dot(left, right):
    return jnp.dot(left, right, preferred_element_type=F32)


def dot_t(left, right):
    return lax.dot_general(left, right, (((1,), (1,)), ((), ())), preferred_element_type=F32)


def head(values, index, size):
    return values[:, index * size : (index + 1) * size]


def with_ones(values):
    return jnp.concatenate([values, jnp.ones(values.shape, values.dtype)], axis=1)


def same_block(rows, levels):
    row = lax.broadcasted_iota(jnp.int32, (rows, rows), 0) // levels
    col = lax.broadcasted_iota(jnp.int32, (rows, rows), 1) // levels
    return row == col


def project(values, squares, weights, scale, size, first=0):
    joined = dot(values, weights)
    inverse = lax.rsqrt(squares)
    floor = squares * EPSILON
    out = []
    for part in range(3 * HEADS - first * HEADS):
        kind = part // HEADS + first
        piece = head(joined, part, size)
        if kind == 2:
            out.append((piece * inverse).astype(BF))
        else:
            factor = lax.rsqrt(jnp.mean(piece * piece, axis=-1, keepdims=True) + floor)
            out.append((piece * (factor * scale if kind == 0 else factor)).astype(BF))
    return [out[i : i + HEADS] for i in range(0, len(out), HEADS)]


def mean_square(values):
    return jnp.mean(values * values, axis=-1, keepdims=True) + EPSILON


def vertical(block, w_vqkv, w_vout, levels):
    rows, width = block.shape
    size = width // HEADS
    scale = math.log2(math.e) / math.sqrt(size)
    values = block.astype(F32)
    heads = range(HEADS)
    keys = dot(block, w_vqkv[:, width : 2 * width])
    queries = dot(block, w_vqkv[:, :width])
    vals = dot(block, w_vqkv[:, 2 * width :])
    squares = mean_square(values)
    squares_k = dot_t(jnp.full((8, width), 1.0 / width, BF), (values * values).astype(BF))[0:1]
    floor, floor_k = squares * EPSILON, (squares_k + EPSILON) * EPSILON
    keys_sq = (keys * keys).astype(BF)
    queries_b, keys_b = queries.astype(BF), keys.astype(BF)
    scores = [dot_t(head(queries_b, h, size), head(keys_b, h, size)) for h in heads]
    ones = jnp.full((8, size), 1.0 / size, BF)
    means_k = [dot_t(ones, head(keys_sq, h, size))[0:1] for h in heads]
    norms_q = [
        lax.rsqrt(jnp.mean(q * q, axis=-1, keepdims=True) + floor) * scale
        for q in (head(queries, h, size) for h in heads)
    ]
    norms_k = [lax.rsqrt(m + floor_k) for m in means_k]
    vals = (vals * lax.rsqrt(squares)).astype(BF)
    expons = [jnp.exp2(x * q * k) for x, q, k in zip(scores, norms_q, norms_k)]
    if rows > levels:
        inside = same_block(rows, levels)
        expons = [jnp.where(inside, e, 0.0) for e in expons]
    totals = [dot(e.astype(BF), with_ones(head(vals, h, size))) for h, e in enumerate(expons)]
    parts = [(t[:, :size] / t[:, size:]).astype(BF) for t in totals]
    return (values + dot(jnp.concatenate(parts, axis=1), w_vout[...])).astype(BF)


def gate_kernel(*refs):
    pass


def early_kernel(levels, *refs):
    operands, outputs, loaded, mixed_s, sems = refs[:6], refs[7:13], refs[14:20], refs[20], refs[21]

    @pl.when(lax.axis_index("tile") == 0)
    def _():
        copies = [
            pltpu.make_async_copy(a, b, sems.at[i]) for i, (a, b) in enumerate(zip(operands, loaded))
        ]
        for copy in copies:
            copy.start()
        own_blocks(levels, *loaded, *outputs, mixed_s, copies)


def late_kernel(levels, *refs):
    @pl.when(lax.axis_index("tile") != 0)
    def _():
        own_blocks(levels, *refs[:6], *refs[12:18], refs[18], ())


def own_blocks(
    levels, x_ref, w_vqkv, w_vout, wet_ref, w_hqkv, w_hout,
    result_ref, mixed_e, query_e, num_e, den_e, pick_ref, mixed_s, copies,
):
    total_rows, width = x_ref.shape
    size = width // HEADS
    scale = math.log2(math.e) / math.sqrt(size)
    blocks = total_rows // levels
    chunk = min(levels, 16)
    edges = [b for b in range(blocks) if b % CB in (0, CB - 1)]
    tile = lax.axis_index("tile")
    tiles = lax.axis_size("tile")
    group = min(max(levels, 128), total_rows)

    def mix(index):
        rows = rows_at(index * group, group)
        mixed_s[rows, :] = vertical(x_ref[rows, :], w_vqkv, w_vout, levels)

    for copy in copies[:3]:
        copy.wait()
    each(total_rows // group, mix)
    for copy in copies[3:]:
        copy.wait()

    rows = blocks * chunk
    row = lax.broadcasted_iota(jnp.int32, (rows, rows), 0)
    col = lax.broadcasted_iota(jnp.int32, (rows, rows), 1)
    block_q, block_k = row // chunk, col // chunk
    wet = jnp.broadcast_to(wet_ref[...], (8, wet_ref.shape[1])).astype(BF)
    which = lax.broadcasted_iota(jnp.int32, (wet.shape[1], rows), 0)
    column = lax.broadcasted_iota(jnp.int32, (wet.shape[1], rows), 1) // chunk
    wet_k = dot(wet, (which == tile * blocks + column).astype(BF))[0:1, :]
    left = lax.rem(tile + tiles - 1, tiles) * blocks + CB - 1
    right = lax.rem(tile + 1, tiles) * blocks
    for i, block in enumerate((left, right)):
        pick_ref[i, :, :] = dot(wet, (which[:, :128] == block).astype(BF))
    near = jnp.abs(block_q % CB - block_k % CB) <= 1
    near = near & (jnp.abs(block_q // CB - block_k // CB) <= 1)
    allowed = (row % chunk == col % chunk) & ((block_q == block_k) | (near & (wet_k > 0.5)))

    def attend(index):
        def spots(b):
            return rows_at(b * levels + index * chunk, chunk)

        mixed = jnp.concatenate([mixed_s[spots(b), :] for b in range(blocks)], axis=0)
        values = mixed.astype(F32)
        queries, keys, vals = project(mixed, mean_square(values), w_hqkv[...], scale, size)
        expons = [jnp.exp2(dot_t(q, k)) for q, k in zip(queries, keys)]
        expons = [jnp.where(allowed, e, 0.0).astype(BF) for e in expons]
        totals = [dot(e, with_ones(v)) for e, v in zip(expons, vals)]
        parts = [(t[:, :size] / t[:, size:]).astype(BF) for t in totals]
        for h, total in enumerate(totals):
            cols = slice(h * size, (h + 1) * size)
            for e, b in enumerate(edges):
                here = slice(b * chunk, (b + 1) * chunk)
                there = rows_at(e * levels + index * chunk, chunk)
                query_e[there, cols] = queries[h][here]
                num_e[there, cols] = total[here, :size]
                den_e[there, cols] = total[here, size:]
        result = (values + dot(jnp.concatenate(parts, axis=1), w_hout[...])).astype(BF)
        for b in range(blocks):
            here = slice(b * chunk, (b + 1) * chunk)
            if b in edges:
                mixed_e[rows_at(edges.index(b) * levels + index * chunk, chunk), :] = mixed[here]
            else:
                result_ref[spots(b), :] = result[here]

    each(levels // chunk, attend)


def halo_kernel(
    levels, blocks, from_left, from_right, pick_ref, mixed_e, query_e, num_e, den_e,
    w_vqkv, w_vout, w_hqkv, w_hout, inner_ref, out_ref, keys_s, values_s, floor_s, result_s, sems,
):
    width = mixed_e.shape[1]
    size = width // HEADS
    chunk = min(levels, 16)
    edges = [b for b in range(blocks) if b % CB in (0, CB - 1)]
    group = 2 * levels if 2 * levels <= 128 else levels
    inner = [
        pltpu.make_async_copy(ref, out_ref.at[pl.ds(b * levels, levels), :], sems.at[b])
        for b in range(blocks) if b not in edges
        for ref in [inner_ref.at[pl.ds(b * levels, levels), :]]
    ]
    for copy in inner:
        copy.start()

    halo = jnp.concatenate(
        [
            jnp.where(pick_ref[i, 0:1, 0:1] > 0.5, ref[0:levels, :], ref[levels : 2 * levels, :])
            for i, ref in enumerate((from_left, from_right))
        ],
        axis=0,
    )
    for start in range(0, 2 * levels, group):
        rows = slice(start, start + group)
        mixed = vertical(halo[rows], w_vqkv, w_vout, levels)
        squares = mean_square(mixed.astype(F32))
        joined = dot(mixed, w_hqkv[:, width:])
        keys_s[rows, :] = joined[:, :width]
        values_s[rows, :] = joined[:, width:] * lax.rsqrt(squares)
        floor_s[rows, :] = jnp.broadcast_to(squares * EPSILON, (group, 128))

    def attend(index):
        def take(ref, count):
            return jnp.concatenate(
                [ref[rows_at(i * levels + index * chunk, chunk), :] for i in range(count)], axis=0
            )

        def per_edge(values):
            sides = [values[:chunk], values[chunk:]]
            return jnp.concatenate([sides[0 if b % CB == 0 else 1] for b in edges], axis=0)

        keys, values, floor = (take(ref, 2) for ref in (keys_s, values_s, floor_s))
        query, num, den = (take(ref, len(edges)) for ref in (query_e, num_e, den_e))
        product = query.astype(F32) * per_edge(keys)
        squares = keys * keys
        heads = range(HEADS)
        scores = [jnp.sum(head(product, h, size), axis=-1, keepdims=True) for h in heads]
        means = [jnp.mean(head(squares, h, size), axis=-1, keepdims=True) for h in heads]
        norms = [per_edge(lax.rsqrt(m + floor[:, 0:1])) for m in means]
        expons = [jnp.exp2(x * n) for x, n in zip(scores, norms)]
        values = per_edge(values)
        parts = [
            ((head(num, h, size) + e * head(values, h, size)) / (head(den, h, size) + e)).astype(BF)
            for h, e in enumerate(expons)
        ]
        update = dot(jnp.concatenate(parts, axis=1), w_hout[...])
        result = (take(mixed_e, len(edges)).astype(F32) + update).astype(BF)
        for e in range(len(edges)):
            there = rows_at(e * levels + index * chunk, chunk)
            result_s[there, :] = result[e * chunk : (e + 1) * chunk]

    each(levels // chunk, attend)
    copies = [
        pltpu.make_async_copy(
            result_s.at[pl.ds(e * levels, levels), :],
            out_ref.at[pl.ds(b * levels, levels), :],
            sems.at[b],
        )
        for e, b in enumerate(edges)
    ]
    for copy in copies:
        copy.start()
    for copy in inner + copies:
        copy.wait()


def on_device(state, wet, w_vqkv, w_vout, w_hqkv, w_hout):
    tiles = lax.axis_size("tile")
    blocks, levels, width = state.shape
    rows = blocks // CB
    edge_rows = 2 * rows * levels
    limit = (10 << 20) + levels * (256 << 10)
    vmem = pl.BlockSpec(memory_space=pltpu.VMEM)
    hbm = pl.BlockSpec(memory_space=pl.ANY)
    whole = jax.ShapeDtypeStruct((blocks * levels, width), BF)
    strip = state.reshape(rows, CB, levels, width)
    edges = [strip[:, c].reshape(rows * levels, width) for c in (CB - 1, 0)]
    to_right, to_left = pl.pallas_call(
        gate_kernel,
        out_shape=[jax.ShapeDtypeStruct(e.shape, e.dtype) for e in edges],
        in_specs=[vmem] * 2,
        out_specs=[vmem] * 2,
        input_output_aliases={0: 0, 1: 1},
        compiler_params=pltpu.CompilerParams(vmem_limit_bytes=1 << 20),
        cost_estimate=pl.CostEstimate(flops=200 << 30, bytes_accessed=1 << 30, transcendentals=0),
        name="gate",
    )(*edges)
    from_left = lax.ppermute(to_right, "tile", [(i, (i + 1) % tiles) for i in range(tiles)])
    results = (
        whole,
        jax.ShapeDtypeStruct((edge_rows, width), BF),
        jax.ShapeDtypeStruct((edge_rows, width), BF),
        jax.ShapeDtypeStruct((edge_rows, width), F32),
        jax.ShapeDtypeStruct((edge_rows, width), F32),
        jax.ShapeDtypeStruct((2, 8, 128), F32),
    )
    operands = (
        state.reshape(blocks * levels, width), w_vqkv, w_vout, wet.reshape(1, -1), w_hqkv, w_hout
    )
    mixed_s = pltpu.VMEM((blocks * levels, width), BF)
    cost = pl.CostEstimate(
        flops=2 * blocks * levels * width * width * 8, bytes_accessed=8 << 20, transcendentals=0
    )
    *early, to_left = pl.pallas_call(
        functools.partial(early_kernel, levels),
        out_shape=results + (jax.ShapeDtypeStruct(to_left.shape, to_left.dtype),),
        in_specs=[hbm] * 6 + [vmem],
        out_specs=(vmem,) * 7,
        input_output_aliases={6: 6},
        scratch_shapes=[pltpu.VMEM(v.shape, v.dtype) for v in operands]
        + [mixed_s, pltpu.SemaphoreType.DMA((6,))],
        compiler_params=pltpu.CompilerParams(vmem_limit_bytes=limit + (6 << 20)),
        cost_estimate=cost,
        name="early_blocks",
    )(*[pltpu.with_memory_space_constraint(v, pltpu.HBM) for v in operands], to_left)
    from_right = lax.ppermute(to_left, "tile", [(i, (i - 1) % tiles) for i in range(tiles)])

    inner, *edge_values, pick = pl.pallas_call(
        functools.partial(late_kernel, levels),
        out_shape=results,
        in_specs=[vmem] * 12,
        out_specs=(vmem,) * 6,
        input_output_aliases={6 + i: i for i in range(6)},
        scratch_shapes=[mixed_s],
        compiler_params=pltpu.CompilerParams(vmem_limit_bytes=limit),
        cost_estimate=cost,
        name="late_blocks",
    )(*operands, *early)
    updated = pl.pallas_call(
        functools.partial(halo_kernel, levels, blocks),
        out_shape=whole,
        in_specs=[vmem] * 12,
        out_specs=hbm,
        scratch_shapes=[
            pltpu.VMEM((2 * levels, width), F32),
            pltpu.VMEM((2 * levels, width), F32),
            pltpu.VMEM((2 * levels, 128), F32),
            pltpu.VMEM((edge_rows, width), BF),
            pltpu.SemaphoreType.DMA((blocks,)),
        ],
        compiler_params=pltpu.CompilerParams(vmem_limit_bytes=limit),
        name="halo_blocks",
    )(from_left, from_right, pick, *edge_values, w_vqkv, w_vout, w_hqkv, w_hout, inner)
    return updated.reshape(blocks, levels, width)


def solution(mesh):
    in_specs = (P(("grp", "tile"), None, None), P(), P(), P(), P(), P())
    out_specs = P(("grp", "tile"), None, None)
    return jax.shard_map(
        on_device, mesh=mesh, in_specs=in_specs, out_specs=out_specs, check_vma=False
    )
```

```python
import functools
import math

import jax
import jax.numpy as jnp
from jax import lax
from jax.experimental import pallas as pl
from jax.experimental.pallas import tpu as pltpu
from jax.sharding import PartitionSpec as P

HEADS = 4
CB = 4
EPSILON = 1e-06
BF = jnp.bfloat16
F32 = jnp.float32


def each(count, body):
    if count == 1:
        body(0)
    else:
        pl.loop(0, count)(body)


def rows_at(start, size):
    if isinstance(start, int):
        return pl.ds(start, size)
    return pl.ds(pl.multiple_of(start, size), size)


def dot(left, right):
    return jnp.dot(left, right, preferred_element_type=F32)


def dot_t(left, right):
    return lax.dot_general(left, right, (((1,), (1,)), ((), ())), preferred_element_type=F32)


def head(values, index, size):
    return values[:, index * size : (index + 1) * size]


def with_ones(values):
    return jnp.concatenate([values, jnp.ones(values.shape, values.dtype)], axis=1)


def same_block(rows, levels):
    row = lax.broadcasted_iota(jnp.int32, (rows, rows), 0) // levels
    col = lax.broadcasted_iota(jnp.int32, (rows, rows), 1) // levels
    return row == col


def project(values, squares, weights, scale, size, first=0):
    joined = dot(values, weights)
    inverse = lax.rsqrt(squares)
    floor = squares * EPSILON
    out = []
    for part in range(3 * HEADS - first * HEADS):
        kind = part // HEADS + first
        piece = head(joined, part, size)
        if kind == 2:
            out.append((piece * inverse).astype(BF))
        else:
            factor = lax.rsqrt(jnp.mean(piece * piece, axis=-1, keepdims=True) + floor)
            out.append((piece * (factor * scale if kind == 0 else factor)).astype(BF))
    return [out[i : i + HEADS] for i in range(0, len(out), HEADS)]


def mean_square(values):
    return jnp.mean(values * values, axis=-1, keepdims=True) + EPSILON


def vertical_context(block, w_vqkv, levels):
    rows, width = block.shape
    size = width // HEADS
    scale = math.log2(math.e) / math.sqrt(size)
    values = block.astype(F32)
    heads = range(HEADS)
    keys = dot(block, w_vqkv[:, width : 2 * width])
    queries = dot(block, w_vqkv[:, :width])
    vals = dot(block, w_vqkv[:, 2 * width :])
    squares = mean_square(values)
    squares_k = dot_t(jnp.full((8, width), 1.0 / width, BF), (values * values).astype(BF))[0:1]
    floor, floor_k = squares * EPSILON, (squares_k + EPSILON) * EPSILON
    keys_sq = (keys * keys).astype(BF)
    queries_b, keys_b = queries.astype(BF), keys.astype(BF)
    scores = [dot_t(head(queries_b, h, size), head(keys_b, h, size)) for h in heads]
    ones = jnp.full((8, size), 1.0 / size, BF)
    means_k = [dot_t(ones, head(keys_sq, h, size))[0:1] for h in heads]
    norms_q = [
        lax.rsqrt(jnp.mean(q * q, axis=-1, keepdims=True) + floor) * scale
        for q in (head(queries, h, size) for h in heads)
    ]
    norms_k = [lax.rsqrt(m + floor_k) for m in means_k]
    vals = (vals * lax.rsqrt(squares)).astype(BF)
    expons = [jnp.exp2(x * q * k) for x, q, k in zip(scores, norms_q, norms_k)]
    if rows > levels:
        inside = same_block(rows, levels)
        expons = [jnp.where(inside, e, 0.0) for e in expons]
    totals = [dot(e.astype(BF), with_ones(head(vals, h, size))) for h, e in enumerate(expons)]
    parts = [(t[:, :size] / t[:, size:]).astype(BF) for t in totals]
    return jnp.concatenate(parts, axis=1)


def edge_kernel(levels, wet_hbm, x_hbm, to_right, to_left, wet_ref, held, sems):
    blocks = x_hbm.shape[0] // levels
    tile = lax.axis_index("tile")
    copies = [pltpu.make_async_copy(wet_hbm, wet_ref, sems.at[4])]
    for i, b in enumerate((CB - 1, 2 * CB - 1, 0, CB)):
        source = x_hbm.at[pl.ds(b * levels, levels), :]
        copies.append(pltpu.make_async_copy(source, held.at[i], sems.at[i]))
    for copy in copies:
        copy.start()
    for copy in copies:
        copy.wait()
    for i, (out_ref, column) in enumerate(((to_right, CB - 1), (to_left, 0))):
        out_ref[...] = jnp.where(wet_ref[0, tile * blocks + column] > 0, held[2 * i], held[2 * i + 1])


def early_kernel(levels, *refs):
    operands, outputs, loaded, mixed_s, sems = refs[:6], refs[7:12], refs[13:19], refs[19], refs[20]

    @pl.when(lax.axis_index("tile") == 0)
    def _():
        copies = [
            pltpu.make_async_copy(a, b, sems.at[i]) for i, (a, b) in enumerate(zip(operands, loaded))
        ]
        for copy in copies:
            copy.start()
        own_blocks(levels, *loaded, *outputs, mixed_s, copies)


def late_kernel(levels, *refs):
    @pl.when(lax.axis_index("tile") != 0)
    def _():
        own_blocks(levels, *refs[:6], *refs[11:16], refs[16], ())


def own_blocks(
    levels, x_ref, w_vqkv, w_vout, wet_ref, w_hqkv, w_hout,
    result_ref, base_e, query_e, term_e, den_e, mixed_s, copies,
):
    total_rows, width = x_ref.shape
    size = width // HEADS
    scale = math.log2(math.e) / math.sqrt(size)
    blocks = total_rows // levels
    chunk = min(levels, 16)
    edges = [b for b in range(blocks) if b % CB in (0, CB - 1)]
    tile = lax.axis_index("tile")
    group = min(max(levels, 128), total_rows)

    def mix(index):
        rows = rows_at(index * group, group)
        block = x_ref[rows, :]
        context = vertical_context(block, w_vqkv, levels)
        mixed_s[rows, :] = (block.astype(F32) + dot(context, w_vout[...])).astype(BF)

    for copy in copies[:3]:
        copy.wait()
    each(total_rows // group, mix)
    for copy in copies[3:]:
        copy.wait()

    rows = blocks * chunk
    row = lax.broadcasted_iota(jnp.int32, (rows, rows), 0)
    col = lax.broadcasted_iota(jnp.int32, (rows, rows), 1)
    block_q, block_k = row // chunk, col // chunk
    wet = jnp.broadcast_to(wet_ref[...], (8, wet_ref.shape[1])).astype(BF)
    which = lax.broadcasted_iota(jnp.int32, (wet.shape[1], rows), 0)
    column = lax.broadcasted_iota(jnp.int32, (wet.shape[1], rows), 1) // chunk
    wet_k = dot(wet, (which == tile * blocks + column).astype(BF))[0:1, :]
    near = jnp.abs(block_q % CB - block_k % CB) <= 1
    near = near & (jnp.abs(block_q // CB - block_k // CB) <= 1)
    allowed = (row % chunk == col % chunk) & ((block_q == block_k) | (near & (wet_k > 0.5)))

    def attend(index):
        def spots(b):
            return rows_at(b * levels + index * chunk, chunk)

        mixed = jnp.concatenate([mixed_s[spots(b), :] for b in range(blocks)], axis=0)
        values = mixed.astype(F32)
        queries, keys, vals = project(mixed, mean_square(values), w_hqkv[...], scale, size)
        expons = [jnp.exp2(dot_t(q, k)) for q, k in zip(queries, keys)]
        expons = [jnp.where(allowed, e, 0.0).astype(BF) for e in expons]
        totals = [dot(e, with_ones(v)) for e, v in zip(expons, vals)]
        parts = [(t[:, :size] / t[:, size:]).astype(BF) for t in totals]
        inner = [b for b in range(blocks) if b not in edges]

        def some(array, which):
            return jnp.concatenate([array[b * chunk : (b + 1) * chunk] for b in which], axis=0)

        context = jnp.concatenate([some(p, inner) for p in parts], axis=1)
        result = (some(values, inner) + dot(context, w_hout[...])).astype(BF)
        terms = [
            dot(some(p, edges), w_hout[h * size : (h + 1) * size, :]) for h, p in enumerate(parts)
        ]
        base = some(values, edges) + sum(terms)
        for i, b in enumerate(inner):
            result_ref[spots(b), :] = result[i * chunk : (i + 1) * chunk]
        for e, b in enumerate(edges):
            here = slice(e * chunk, (e + 1) * chunk)
            there = rows_at(e * levels + index * chunk, chunk)
            base_e[there, :] = base[here]
            for h in range(HEADS):
                cols = slice(h * size, (h + 1) * size)
                query_e[there, cols] = queries[h][b * chunk : (b + 1) * chunk].astype(F32)
                den_e[there, cols] = totals[h][b * chunk : (b + 1) * chunk, size:]
                term_e[h, there, :] = terms[h][here]

    each(levels // chunk, attend)


def halo_kernel(
    levels, blocks, from_left, from_right, base_e, query_e, term_e, den_e,
    w_vqkv, w_vout, w_hqkv, w_hout, inner_ref, out_ref, result_s, sems,
):
    width = base_e.shape[1]
    size = width // HEADS
    chunk = min(levels, 16)
    edges = [b for b in range(blocks) if b % CB in (0, CB - 1)]
    group = 2 * levels if 2 * levels <= 128 else levels
    inner = [
        pltpu.make_async_copy(ref, out_ref.at[pl.ds(b * levels, levels), :], sems.at[b])
        for b in range(blocks) if b not in edges
        for ref in [inner_ref.at[pl.ds(b * levels, levels), :]]
    ]
    for copy in inner:
        copy.start()

    halo = jnp.concatenate([from_left[...], from_right[...]], axis=0)
    heads = range(HEADS)
    pieces = []
    for start in range(0, 2 * levels, group):
        block = halo[start : start + group]
        context = vertical_context(block, w_vqkv, levels)
        mixed = (block.astype(F32) + dot(context, w_vout[...])).astype(BF)
        joined = dot(mixed, w_hqkv[:, width:])
        mixed = mixed.astype(F32)
        squares = mean_square(mixed)
        values = (joined[:, width:] * lax.rsqrt(squares)).astype(BF)
        moved = [
            dot(head(values, h, size), w_hout[h * size : (h + 1) * size, :]) for h in heads
        ]
        pieces.append((joined[:, :width], squares * EPSILON, *moved))
    keys, floor, *moved = (jnp.concatenate(p, axis=0) for p in zip(*pieces))

    for index in range(levels // chunk):
        def take(source, count):
            return jnp.concatenate(
                [source[i * levels + index * chunk :][:chunk] for i in range(count)], axis=0
            )

        def per_edge(values):
            sides = [values[:chunk], values[chunk:]]
            return jnp.concatenate([sides[0 if b % CB == 0 else 1] for b in edges], axis=0)

        def edge(*spot):
            return jnp.concatenate(
                [
                    ref[(*lead, pl.ds(e * levels + index * chunk, chunk), slice(None))]
                    for ref, *lead in [spot]
                    for e in range(len(edges))
                ],
                axis=0,
            )

        chunk_keys, chunk_floor = take(keys, 2), take(floor, 2)
        product = edge(query_e) * per_edge(chunk_keys)
        squares = chunk_keys * chunk_keys
        scores = [jnp.sum(head(product, h, size), axis=-1, keepdims=True) for h in heads]
        means = [jnp.mean(head(squares, h, size), axis=-1, keepdims=True) for h in heads]
        norms = [per_edge(lax.rsqrt(m + chunk_floor)) for m in means]
        expons = [jnp.exp2(x * n) for x, n in zip(scores, norms)]
        den = edge(den_e)
        shares = [e / (den[:, h * size : h * size + 1] + e) for h, e in enumerate(expons)]
        result = edge(base_e)
        for h, share in enumerate(shares):
            result = result + share * (per_edge(take(moved[h], 2)) - edge(term_e, h))
        result = result.astype(BF)
        for e in range(len(edges)):
            there = pl.ds(e * levels + index * chunk, chunk)
            result_s[there, :] = result[e * chunk : (e + 1) * chunk]

    copies = [
        pltpu.make_async_copy(
            result_s.at[pl.ds(e * levels, levels), :],
            out_ref.at[pl.ds(b * levels, levels), :],
            sems.at[b],
        )
        for e, b in enumerate(edges)
    ]
    for copy in copies:
        copy.start()
    for copy in inner + copies:
        copy.wait()


def on_device(state, wet, w_vqkv, w_vout, w_hqkv, w_hout):
    tiles = lax.axis_size("tile")
    blocks, levels, width = state.shape
    rows = blocks // CB
    edge_rows = 2 * rows * levels
    limit = (10 << 20) + levels * (256 << 10)
    vmem = pl.BlockSpec(memory_space=pltpu.VMEM)
    hbm = pl.BlockSpec(memory_space=pl.ANY)
    whole = jax.ShapeDtypeStruct((blocks * levels, width), BF)
    flat = state.reshape(blocks * levels, width)
    one = jax.ShapeDtypeStruct((levels, width), BF)
    to_right, to_left = pl.pallas_call(
        functools.partial(edge_kernel, levels),
        out_shape=(one, one),
        in_specs=[hbm] * 2,
        out_specs=(vmem,) * 2,
        scratch_shapes=[pltpu.SMEM((1, wet.shape[0]), wet.dtype), pltpu.VMEM((4, levels, width), BF), pltpu.SemaphoreType.DMA((5,))],
        compiler_params=pltpu.CompilerParams(vmem_limit_bytes=4 << 20),
        cost_estimate=pl.CostEstimate(flops=200 << 30, bytes_accessed=1 << 30, transcendentals=0),
        name="edge_blocks",
    )(*[pltpu.with_memory_space_constraint(v, pltpu.HBM) for v in (wet.reshape(1, -1), flat)])
    from_left = lax.ppermute(to_right, "tile", [(i, (i + 1) % tiles) for i in range(tiles)])
    edge_f32 = jax.ShapeDtypeStruct((edge_rows, width), F32)
    results = (
        whole,
        edge_f32,
        edge_f32,
        jax.ShapeDtypeStruct((HEADS, edge_rows, width), F32),
        edge_f32,
    )
    operands = (
        state.reshape(blocks * levels, width), w_vqkv, w_vout, wet.reshape(1, -1), w_hqkv, w_hout
    )
    mixed_s = pltpu.VMEM((blocks * levels, width), BF)
    cost = pl.CostEstimate(
        flops=2 * blocks * levels * width * width * 8, bytes_accessed=8 << 20, transcendentals=0
    )
    *early, to_left = pl.pallas_call(
        functools.partial(early_kernel, levels),
        out_shape=results + (jax.ShapeDtypeStruct(to_left.shape, to_left.dtype),),
        in_specs=[hbm] * 6 + [vmem],
        out_specs=(vmem,) * 6,
        input_output_aliases={6: 5},
        scratch_shapes=[pltpu.VMEM(v.shape, v.dtype) for v in operands]
        + [mixed_s, pltpu.SemaphoreType.DMA((6,))],
        compiler_params=pltpu.CompilerParams(vmem_limit_bytes=limit + (6 << 20)),
        cost_estimate=cost,
        name="early_blocks",
    )(*[pltpu.with_memory_space_constraint(v, pltpu.HBM) for v in operands], to_left)
    from_right = lax.ppermute(to_left, "tile", [(i, (i - 1) % tiles) for i in range(tiles)])

    inner, *edge_values = pl.pallas_call(
        functools.partial(late_kernel, levels),
        out_shape=results,
        in_specs=[vmem] * 11,
        out_specs=(vmem,) * 5,
        input_output_aliases={6 + i: i for i in range(5)},
        scratch_shapes=[mixed_s],
        compiler_params=pltpu.CompilerParams(vmem_limit_bytes=limit),
        cost_estimate=cost,
        name="late_blocks",
    )(*operands, *early)
    updated = pl.pallas_call(
        functools.partial(halo_kernel, levels, blocks),
        out_shape=whole,
        in_specs=[vmem] * 11,
        out_specs=hbm,
        scratch_shapes=[
            pltpu.VMEM((edge_rows, width), BF),
            pltpu.SemaphoreType.DMA((blocks,)),
        ],
        compiler_params=pltpu.CompilerParams(vmem_limit_bytes=limit),
        name="halo_blocks",
    )(from_left, from_right, *edge_values, w_vqkv, w_vout, w_hqkv, w_hout, inner)
    return updated.reshape(blocks, levels, width)


def solution(mesh):
    in_specs = (P(("grp", "tile"), None, None), P(), P(), P(), P(), P())
    out_specs = P(("grp", "tile"), None, None)
    return jax.shard_map(
        on_device, mesh=mesh, in_specs=in_specs, out_specs=out_specs, check_vma=False
    )
```

```python
import functools
import math

import jax
import jax.numpy as jnp
from jax import lax
from jax.experimental import pallas as pl
from jax.experimental.pallas import tpu as pltpu
from jax.sharding import PartitionSpec as P

HEADS = 4
CB = 4
EPSILON = 1e-06
BF = jnp.bfloat16
F32 = jnp.float32


def each(count, body):
    if count == 1:
        body(0)
    else:
        pl.loop(0, count)(body)


def rows_at(start, size):
    if isinstance(start, int):
        return pl.ds(start, size)
    return pl.ds(pl.multiple_of(start, size), size)


def dot(left, right):
    return jnp.dot(left, right, preferred_element_type=F32)


def dot_t(left, right):
    return lax.dot_general(left, right, (((1,), (1,)), ((), ())), preferred_element_type=F32)


def head(values, index, size):
    return values[:, index * size : (index + 1) * size]


def with_ones(values):
    return jnp.concatenate([values, jnp.ones(values.shape, values.dtype)], axis=1)


def same_block(rows, levels):
    row = lax.broadcasted_iota(jnp.int32, (rows, rows), 0) // levels
    col = lax.broadcasted_iota(jnp.int32, (rows, rows), 1) // levels
    return row == col


def project(values, squares, weights, scale, size, first=0):
    joined = dot(values, weights)
    inverse = lax.rsqrt(squares)
    floor = squares * EPSILON
    out = []
    for part in range(3 * HEADS - first * HEADS):
        kind = part // HEADS + first
        piece = head(joined, part, size)
        if kind == 2:
            out.append((piece * inverse).astype(BF))
        else:
            factor = lax.rsqrt(jnp.mean(piece * piece, axis=-1, keepdims=True) + floor)
            out.append((piece * (factor * scale if kind == 0 else factor)).astype(BF))
    return [out[i : i + HEADS] for i in range(0, len(out), HEADS)]


def mean_square(values):
    return jnp.mean(values * values, axis=-1, keepdims=True) + EPSILON


def vertical_context(block, w_vqkv, levels):
    rows, width = block.shape
    size = width // HEADS
    scale = math.log2(math.e) / math.sqrt(size)
    values = block.astype(F32)
    heads = range(HEADS)
    keys = dot(block, w_vqkv[:, width : 2 * width])
    queries = dot(block, w_vqkv[:, :width])
    vals = dot(block, w_vqkv[:, 2 * width :])
    squares = mean_square(values)
    squares_k = dot_t(jnp.full((8, width), 1.0 / width, BF), (values * values).astype(BF))[0:1]
    floor, floor_k = squares * EPSILON, (squares_k + EPSILON) * EPSILON
    keys_sq = (keys * keys).astype(BF)
    queries_b, keys_b = queries.astype(BF), keys.astype(BF)
    scores = [dot_t(head(queries_b, h, size), head(keys_b, h, size)) for h in heads]
    ones = jnp.full((8, size), 1.0 / size, BF)
    means_k = [dot_t(ones, head(keys_sq, h, size))[0:1] for h in heads]
    norms_q = [
        lax.rsqrt(jnp.mean(q * q, axis=-1, keepdims=True) + floor) * scale
        for q in (head(queries, h, size) for h in heads)
    ]
    norms_k = [lax.rsqrt(m + floor_k) for m in means_k]
    vals = (vals * lax.rsqrt(squares)).astype(BF)
    expons = [jnp.exp2(x * q * k) for x, q, k in zip(scores, norms_q, norms_k)]
    if rows > levels:
        inside = same_block(rows, levels)
        expons = [jnp.where(inside, e, 0.0) for e in expons]
    totals = [dot(e.astype(BF), with_ones(head(vals, h, size))) for h, e in enumerate(expons)]
    parts = [(t[:, :size] / t[:, size:]).astype(BF) for t in totals]
    return jnp.concatenate(parts, axis=1)


def edge_kernel(wet_hbm, x_hbm, to_right, to_left, wet_ref, held, sems):
    blocks = x_hbm.shape[0] * CB
    tile = lax.axis_index("tile")
    copies = [
        pltpu.make_async_copy(wet_hbm, wet_ref, sems.at[0]),
        pltpu.make_async_copy(x_hbm.at[:, CB - 1], held.at[0], sems.at[1]),
        pltpu.make_async_copy(x_hbm.at[:, 0], held.at[1], sems.at[2]),
    ]
    for copy in copies:
        copy.start()
    for copy in copies:
        copy.wait()
    for i, (out_ref, column) in enumerate(((to_right, CB - 1), (to_left, 0))):
        out_ref[...] = jnp.where(wet_ref[0, tile * blocks + column] > 0, held[i, 0], held[i, 1])


def early_kernel(levels, *refs):
    operands, outputs = refs[:6], refs[7:12]

    def run(*scratch):
        *loaded, mixed_s, sems = scratch
        copies = [
            pltpu.make_async_copy(a, b, sems.at[i]) for i, (a, b) in enumerate(zip(operands, loaded))
        ]
        for copy in copies:
            copy.start()
        own_blocks(levels, *loaded, *outputs, mixed_s, copies)

    @pl.when(lax.axis_index("tile") == 0)
    def _():
        pl.run_scoped(
            run,
            *[pltpu.VMEM(ref.shape, ref.dtype) for ref in operands],
            pltpu.VMEM(operands[0].shape, BF),
            pltpu.SemaphoreType.DMA((len(operands),)),
        )


def late_kernel(levels, *refs):
    @pl.when(lax.axis_index("tile") != 0)
    def _():
        own_blocks(levels, *refs[:6], *refs[11:16], refs[16], ())


def own_blocks(
    levels, x_ref, w_vqkv, w_vout, wet_ref, w_hqkv, w_hout,
    result_ref, base_e, query_e, term_e, den_e, mixed_s, copies,
):
    total_rows, width = x_ref.shape
    size = width // HEADS
    scale = math.log2(math.e) / math.sqrt(size)
    blocks = total_rows // levels
    chunk = min(levels, 16)
    edges = [b for b in range(blocks) if b % CB in (0, CB - 1)]
    tile = lax.axis_index("tile")
    group = min(max(levels, 128), total_rows)

    def mix(index):
        rows = rows_at(index * group, group)
        block = x_ref[rows, :]
        context = vertical_context(block, w_vqkv, levels)
        mixed_s[rows, :] = (block.astype(F32) + dot(context, w_vout[...])).astype(BF)

    for copy in copies[:3]:
        copy.wait()
    each(total_rows // group, mix)
    for copy in copies[3:]:
        copy.wait()

    rows = blocks * chunk
    row = lax.broadcasted_iota(jnp.int32, (rows, rows), 0)
    col = lax.broadcasted_iota(jnp.int32, (rows, rows), 1)
    block_q, block_k = row // chunk, col // chunk
    wet = jnp.broadcast_to(wet_ref[...], (8, wet_ref.shape[1])).astype(BF)
    which = lax.broadcasted_iota(jnp.int32, (wet.shape[1], rows), 0)
    column = lax.broadcasted_iota(jnp.int32, (wet.shape[1], rows), 1) // chunk
    wet_k = dot(wet, (which == tile * blocks + column).astype(BF))[0:1, :]
    near = jnp.abs(block_q % CB - block_k % CB) <= 1
    near = near & (jnp.abs(block_q // CB - block_k // CB) <= 1)
    allowed = (row % chunk == col % chunk) & ((block_q == block_k) | (near & (wet_k > 0.5)))

    def attend(index):
        def spots(b):
            return rows_at(b * levels + index * chunk, chunk)

        mixed = jnp.concatenate([mixed_s[spots(b), :] for b in range(blocks)], axis=0)
        values = mixed.astype(F32)
        queries, keys, vals = project(mixed, mean_square(values), w_hqkv[...], scale, size)
        expons = [jnp.exp2(dot_t(q, k)) for q, k in zip(queries, keys)]
        expons = [jnp.where(allowed, e, 0.0).astype(BF) for e in expons]
        totals = [dot(e, with_ones(v)) for e, v in zip(expons, vals)]
        parts = [(t[:, :size] / t[:, size:]).astype(BF) for t in totals]
        inner = [b for b in range(blocks) if b not in edges]

        def some(array, which):
            return jnp.concatenate([array[b * chunk : (b + 1) * chunk] for b in which], axis=0)

        context = jnp.concatenate([some(p, inner) for p in parts], axis=1)
        result = (some(values, inner) + dot(context, w_hout[...])).astype(BF)
        terms = [
            dot(some(p, edges), w_hout[h * size : (h + 1) * size, :]) for h, p in enumerate(parts)
        ]
        base = some(values, edges) + sum(terms)
        for i, b in enumerate(inner):
            result_ref[spots(b), :] = result[i * chunk : (i + 1) * chunk]
        for e, b in enumerate(edges):
            here = slice(e * chunk, (e + 1) * chunk)
            there = rows_at(e * levels + index * chunk, chunk)
            base_e[there, :] = base[here]
            for h in range(HEADS):
                cols = slice(h * size, (h + 1) * size)
                query_e[there, cols] = queries[h][b * chunk : (b + 1) * chunk].astype(F32)
                den_e[there, cols] = totals[h][b * chunk : (b + 1) * chunk, size:]
                term_e[h, there, :] = terms[h][here]

    each(levels // chunk, attend)


def halo_kernel(
    levels, blocks, from_left, from_right, base_e, query_e, term_e, den_e,
    w_vqkv, w_vout, w_hqkv, w_hout, inner_ref, out_ref, result_s, sem,
):
    width = base_e.shape[1]
    size = width // HEADS
    chunk = min(levels, 16)
    edges = [b for b in range(blocks) if b % CB in (0, CB - 1)]
    group = 2 * levels if 2 * levels <= 128 else levels
    for b in range(blocks):
        if b not in edges:
            here = pl.ds(b * levels, levels)
            result_s[here, :] = inner_ref[here, :]

    halo = jnp.concatenate([from_left[...], from_right[...]], axis=0)
    heads = range(HEADS)
    pieces = []
    for start in range(0, 2 * levels, group):
        block = halo[start : start + group]
        context = vertical_context(block, w_vqkv, levels)
        mixed = (block.astype(F32) + dot(context, w_vout[...])).astype(BF)
        joined = dot(mixed, w_hqkv[:, width:])
        mixed = mixed.astype(F32)
        squares = mean_square(mixed)
        values = (joined[:, width:] * lax.rsqrt(squares)).astype(BF)
        moved = [
            dot(head(values, h, size), w_hout[h * size : (h + 1) * size, :]) for h in heads
        ]
        pieces.append((joined[:, :width], squares * EPSILON, *moved))
    keys, floor, *moved = (jnp.concatenate(p, axis=0) for p in zip(*pieces))

    for index in range(levels // chunk):
        def take(source, count):
            return jnp.concatenate(
                [source[i * levels + index * chunk :][:chunk] for i in range(count)], axis=0
            )

        def per_edge(values):
            sides = [values[:chunk], values[chunk:]]
            return jnp.concatenate([sides[0 if b % CB == 0 else 1] for b in edges], axis=0)

        def edge(*spot):
            return jnp.concatenate(
                [
                    ref[(*lead, pl.ds(e * levels + index * chunk, chunk), slice(None))]
                    for ref, *lead in [spot]
                    for e in range(len(edges))
                ],
                axis=0,
            )

        chunk_keys, chunk_floor = take(keys, 2), take(floor, 2)
        product = edge(query_e) * per_edge(chunk_keys)
        squares = chunk_keys * chunk_keys
        scores = [jnp.sum(head(product, h, size), axis=-1, keepdims=True) for h in heads]
        means = [jnp.mean(head(squares, h, size), axis=-1, keepdims=True) for h in heads]
        norms = [per_edge(lax.rsqrt(m + chunk_floor)) for m in means]
        expons = [jnp.exp2(x * n) for x, n in zip(scores, norms)]
        den = edge(den_e)
        shares = [e / (den[:, h * size : h * size + 1] + e) for h, e in enumerate(expons)]
        result = edge(base_e)
        for h, share in enumerate(shares):
            result = result + share * (per_edge(take(moved[h], 2)) - edge(term_e, h))
        result = result.astype(BF)
        for e, b in enumerate(edges):
            there = pl.ds(b * levels + index * chunk, chunk)
            result_s[there, :] = result[e * chunk : (e + 1) * chunk]

    copy = pltpu.make_async_copy(result_s, out_ref, sem)
    copy.start()
    copy.wait()


def on_device(state, wet, w_vqkv, w_vout, w_hqkv, w_hout):
    tiles = lax.axis_size("tile")
    blocks, levels, width = state.shape
    rows = blocks // CB
    edge_rows = 2 * rows * levels
    limit = (10 << 20) + levels * (256 << 10)
    vmem = pl.BlockSpec(memory_space=pltpu.VMEM)
    hbm = pl.BlockSpec(memory_space=pl.ANY)
    whole = jax.ShapeDtypeStruct((blocks * levels, width), BF)
    strip = state.reshape(rows, CB, levels, width)
    one = jax.ShapeDtypeStruct((levels, width), BF)
    to_right, to_left = pl.pallas_call(
        edge_kernel,
        out_shape=(one, one),
        in_specs=[hbm] * 2,
        out_specs=(vmem,) * 2,
        scratch_shapes=[
            pltpu.SMEM((1, wet.shape[0]), wet.dtype),
            pltpu.VMEM((2, rows, levels, width), BF),
            pltpu.SemaphoreType.DMA((3,)),
        ],
        compiler_params=pltpu.CompilerParams(vmem_limit_bytes=4 << 20),
        cost_estimate=pl.CostEstimate(flops=200 << 30, bytes_accessed=1 << 30, transcendentals=0),
        name="edge_blocks",
    )(*[pltpu.with_memory_space_constraint(v, pltpu.HBM) for v in (wet.reshape(1, -1), strip)])
    from_left = lax.ppermute(to_right, "tile", [(i, (i + 1) % tiles) for i in range(tiles)])
    edge_f32 = jax.ShapeDtypeStruct((edge_rows, width), F32)
    results = (
        whole,
        edge_f32,
        edge_f32,
        jax.ShapeDtypeStruct((HEADS, edge_rows, width), F32),
        edge_f32,
    )
    operands = (
        state.reshape(blocks * levels, width), w_vqkv, w_vout, wet.reshape(1, -1), w_hqkv, w_hout
    )
    mixed_s = pltpu.VMEM((blocks * levels, width), BF)
    cost = pl.CostEstimate(
        flops=2 * blocks * levels * width * width * 8, bytes_accessed=8 << 20, transcendentals=0
    )
    *early, to_left = pl.pallas_call(
        functools.partial(early_kernel, levels),
        out_shape=results + (jax.ShapeDtypeStruct(to_left.shape, to_left.dtype),),
        in_specs=[hbm] * 6 + [vmem],
        out_specs=(vmem,) * 6,
        input_output_aliases={6: 5},
        compiler_params=pltpu.CompilerParams(vmem_limit_bytes=limit + (6 << 20)),
        cost_estimate=cost,
        name="early_blocks",
    )(*[pltpu.with_memory_space_constraint(v, pltpu.HBM) for v in operands], to_left)
    from_right = lax.ppermute(to_left, "tile", [(i, (i - 1) % tiles) for i in range(tiles)])

    inner, *edge_values = pl.pallas_call(
        functools.partial(late_kernel, levels),
        out_shape=results,
        in_specs=[vmem] * 11,
        out_specs=(vmem,) * 5,
        input_output_aliases={6 + i: i for i in range(5)},
        scratch_shapes=[mixed_s],
        compiler_params=pltpu.CompilerParams(vmem_limit_bytes=limit),
        cost_estimate=cost,
        name="late_blocks",
    )(*operands, *early)
    updated = pl.pallas_call(
        functools.partial(halo_kernel, levels, blocks),
        out_shape=whole,
        in_specs=[vmem] * 11,
        out_specs=hbm,
        scratch_shapes=[
            pltpu.VMEM(whole.shape, BF),
            pltpu.SemaphoreType.DMA,
        ],
        compiler_params=pltpu.CompilerParams(vmem_limit_bytes=limit),
        name="halo_blocks",
    )(from_left, from_right, *edge_values, w_vqkv, w_vout, w_hqkv, w_hout, inner)
    return updated.reshape(blocks, levels, width)


def solution(mesh):
    in_specs = (P(("grp", "tile"), None, None), P(), P(), P(), P(), P())
    out_specs = P(("grp", "tile"), None, None)
    return jax.shard_map(
        on_device, mesh=mesh, in_specs=in_specs, out_specs=out_specs, check_vma=False
    )
```

```python
import functools
import math

import jax
import jax.numpy as jnp
from jax import lax
from jax.experimental import pallas as pl
from jax.experimental.pallas import tpu as pltpu
from jax.sharding import PartitionSpec as P

HEADS = 4
CB = 4
EPSILON = 1e-06
BF = jnp.bfloat16
F32 = jnp.float32


def each(count, body):
    if count == 1:
        body(0)
    else:
        pl.loop(0, count)(body)


def rows_at(start, size):
    if isinstance(start, int):
        return pl.ds(start, size)
    return pl.ds(pl.multiple_of(start, size), size)


def dot(left, right):
    return jnp.dot(left, right, preferred_element_type=F32)


def dot_t(left, right):
    return lax.dot_general(left, right, (((1,), (1,)), ((), ())), preferred_element_type=F32)


def head(values, index, size):
    return values[:, index * size : (index + 1) * size]


def with_ones(values):
    return jnp.concatenate([values, jnp.ones(values.shape, values.dtype)], axis=1)


def same_block(rows, levels):
    row = lax.broadcasted_iota(jnp.int32, (rows, rows), 0) // levels
    col = lax.broadcasted_iota(jnp.int32, (rows, rows), 1) // levels
    return row == col


def project(values, squares, weights, scale, size, first=0):
    joined = dot(values, weights)
    inverse = lax.rsqrt(squares)
    floor = squares * EPSILON
    out = []
    for part in range(3 * HEADS - first * HEADS):
        kind = part // HEADS + first
        piece = head(joined, part, size)
        if kind == 2:
            out.append((piece * inverse).astype(BF))
        else:
            factor = lax.rsqrt(jnp.mean(piece * piece, axis=-1, keepdims=True) + floor)
            out.append((piece * (factor * scale if kind == 0 else factor)).astype(BF))
    return [out[i : i + HEADS] for i in range(0, len(out), HEADS)]


def mean_square(values):
    return jnp.mean(values * values, axis=-1, keepdims=True) + EPSILON


def vertical_context(block, w_vqkv, levels):
    rows, width = block.shape
    size = width // HEADS
    scale = math.log2(math.e) / math.sqrt(size)
    values = block.astype(F32)
    heads = range(HEADS)
    keys = dot(block, w_vqkv[:, width : 2 * width])
    queries = dot(block, w_vqkv[:, :width])
    vals = dot(block, w_vqkv[:, 2 * width :])
    squares = mean_square(values)
    squares_k = dot_t(jnp.full((8, width), 1.0 / width, BF), (values * values).astype(BF))[0:1]
    floor, floor_k = squares * EPSILON, (squares_k + EPSILON) * EPSILON
    keys_sq = (keys * keys).astype(BF)
    queries_b, keys_b = queries.astype(BF), keys.astype(BF)
    scores = [dot_t(head(queries_b, h, size), head(keys_b, h, size)) for h in heads]
    ones = jnp.full((8, size), 1.0 / size, BF)
    means_k = [dot_t(ones, head(keys_sq, h, size))[0:1] for h in heads]
    norms_q = [
        lax.rsqrt(jnp.mean(q * q, axis=-1, keepdims=True) + floor) * scale
        for q in (head(queries, h, size) for h in heads)
    ]
    norms_k = [lax.rsqrt(m + floor_k) for m in means_k]
    vals = (vals * lax.rsqrt(squares)).astype(BF)
    expons = [jnp.exp2(x * q * k) for x, q, k in zip(scores, norms_q, norms_k)]
    if rows > levels:
        inside = same_block(rows, levels)
        expons = [jnp.where(inside, e, 0.0) for e in expons]
    totals = [dot(e.astype(BF), with_ones(head(vals, h, size))) for h, e in enumerate(expons)]
    parts = [(t[:, :size] / t[:, size:]).astype(BF) for t in totals]
    return jnp.concatenate(parts, axis=1)


def edge_kernel(wet_hbm, x_hbm, to_right, to_left, wet_ref, held, sems):
    blocks = x_hbm.shape[0] * CB
    tile = lax.axis_index("tile")
    copies = [
        pltpu.make_async_copy(wet_hbm, wet_ref, sems.at[0]),
        pltpu.make_async_copy(x_hbm.at[:, CB - 1], held.at[0], sems.at[1]),
        pltpu.make_async_copy(x_hbm.at[:, 0], held.at[1], sems.at[2]),
    ]
    for copy in copies:
        copy.start()
    for copy in copies:
        copy.wait()
    for i, (out_ref, column) in enumerate(((to_right, CB - 1), (to_left, 0))):
        out_ref[...] = jnp.where(wet_ref[0, tile * blocks + column] > 0, held[i, 0], held[i, 1])


def early_kernel(levels, *refs):
    operands, outputs = refs[:6], refs[7:12]
    refs[12][...] = refs[6][...]

    def run(*scratch):
        *loaded, mixed_s, sems = scratch
        copies = [
            pltpu.make_async_copy(a, b, sems.at[i]) for i, (a, b) in enumerate(zip(operands, loaded))
        ]
        for copy in copies:
            copy.start()
        own_blocks(levels, *loaded, *outputs, mixed_s, copies)

    @pl.when(lax.axis_index("tile") == 0)
    def _():
        pl.run_scoped(
            run,
            *[pltpu.VMEM(ref.shape, ref.dtype) for ref in operands],
            pltpu.VMEM(operands[0].shape, BF),
            pltpu.SemaphoreType.DMA((len(operands),)),
        )


def late_kernel(levels, *refs):
    operands, early, outputs, mixed_s = refs[:6], refs[6:11], refs[11:16], refs[16]

    @pl.when(lax.axis_index("tile") == 0)
    def _():
        for source, target in zip(early, outputs):
            target[...] = source[...]

    @pl.when(lax.axis_index("tile") != 0)
    def _():
        own_blocks(levels, *operands, *outputs, mixed_s, ())


def own_blocks(
    levels, x_ref, w_vqkv, w_vout, wet_ref, w_hqkv, w_hout,
    result_ref, base_e, query_e, term_e, den_e, mixed_s, copies,
):
    total_rows, width = x_ref.shape
    size = width // HEADS
    scale = math.log2(math.e) / math.sqrt(size)
    blocks = total_rows // levels
    chunk = min(levels, 16)
    edges = [b for b in range(blocks) if b % CB in (0, CB - 1)]
    tile = lax.axis_index("tile")
    group = min(max(levels, 128), total_rows)

    def mix(index):
        rows = rows_at(index * group, group)
        block = x_ref[rows, :]
        context = vertical_context(block, w_vqkv, levels)
        mixed_s[rows, :] = (block.astype(F32) + dot(context, w_vout[...])).astype(BF)

    for copy in copies[:3]:
        copy.wait()
    each(total_rows // group, mix)
    for copy in copies[3:]:
        copy.wait()

    rows = blocks * chunk
    row = lax.broadcasted_iota(jnp.int32, (rows, rows), 0)
    col = lax.broadcasted_iota(jnp.int32, (rows, rows), 1)
    block_q, block_k = row // chunk, col // chunk
    wet = jnp.broadcast_to(wet_ref[...], (8, wet_ref.shape[1])).astype(BF)
    which = lax.broadcasted_iota(jnp.int32, (wet.shape[1], rows), 0)
    column = lax.broadcasted_iota(jnp.int32, (wet.shape[1], rows), 1) // chunk
    wet_k = dot(wet, (which == tile * blocks + column).astype(BF))[0:1, :]
    near = jnp.abs(block_q % CB - block_k % CB) <= 1
    near = near & (jnp.abs(block_q // CB - block_k // CB) <= 1)
    allowed = (row % chunk == col % chunk) & ((block_q == block_k) | (near & (wet_k > 0.5)))

    def attend(index):
        def spots(b):
            return rows_at(b * levels + index * chunk, chunk)

        mixed = jnp.concatenate([mixed_s[spots(b), :] for b in range(blocks)], axis=0)
        values = mixed.astype(F32)
        queries, keys, vals = project(mixed, mean_square(values), w_hqkv[...], scale, size)
        expons = [jnp.exp2(dot_t(q, k)) for q, k in zip(queries, keys)]
        expons = [jnp.where(allowed, e, 0.0).astype(BF) for e in expons]
        totals = [dot(e, with_ones(v)) for e, v in zip(expons, vals)]
        parts = [(t[:, :size] / t[:, size:]).astype(BF) for t in totals]
        inner = [b for b in range(blocks) if b not in edges]

        def some(array, which):
            return jnp.concatenate([array[b * chunk : (b + 1) * chunk] for b in which], axis=0)

        context = jnp.concatenate([some(p, inner) for p in parts], axis=1)
        result = (some(values, inner) + dot(context, w_hout[...])).astype(BF)
        terms = [
            dot(some(p, edges), w_hout[h * size : (h + 1) * size, :]) for h, p in enumerate(parts)
        ]
        base = some(values, edges) + sum(terms)
        for i, b in enumerate(inner):
            result_ref[spots(b), :] = result[i * chunk : (i + 1) * chunk]
        for e, b in enumerate(edges):
            here = slice(e * chunk, (e + 1) * chunk)
            there = rows_at(e * levels + index * chunk, chunk)
            base_e[there, :] = base[here]
            for h in range(HEADS):
                cols = slice(h * size, (h + 1) * size)
                query_e[there, cols] = queries[h][b * chunk : (b + 1) * chunk].astype(F32)
                den_e[there, cols] = totals[h][b * chunk : (b + 1) * chunk, size:]
                term_e[h, there, :] = terms[h][here]

    each(levels // chunk, attend)


def halo_kernel(
    levels, blocks, from_left, from_right, base_e, query_e, term_e, den_e,
    w_vqkv, w_vout, w_hqkv, w_hout, inner_ref, out_ref, result_s, sem,
):
    width = base_e.shape[1]
    size = width // HEADS
    chunk = min(levels, 16)
    edges = [b for b in range(blocks) if b % CB in (0, CB - 1)]
    group = 2 * levels if 2 * levels <= 128 else levels
    for b in range(blocks):
        if b not in edges:
            here = pl.ds(b * levels, levels)
            result_s[here, :] = inner_ref[here, :]

    halo = jnp.concatenate([from_left[...], from_right[...]], axis=0)
    heads = range(HEADS)
    pieces = []
    for start in range(0, 2 * levels, group):
        block = halo[start : start + group]
        context = vertical_context(block, w_vqkv, levels)
        mixed = (block.astype(F32) + dot(context, w_vout[...])).astype(BF)
        joined = dot(mixed, w_hqkv[:, width:])
        mixed = mixed.astype(F32)
        squares = mean_square(mixed)
        values = (joined[:, width:] * lax.rsqrt(squares)).astype(BF)
        moved = [
            dot(head(values, h, size), w_hout[h * size : (h + 1) * size, :]) for h in heads
        ]
        pieces.append((joined[:, :width], squares * EPSILON, *moved))
    keys, floor, *moved = (jnp.concatenate(p, axis=0) for p in zip(*pieces))

    for index in range(levels // chunk):
        def take(source, count):
            return jnp.concatenate(
                [source[i * levels + index * chunk :][:chunk] for i in range(count)], axis=0
            )

        def per_edge(values):
            sides = [values[:chunk], values[chunk:]]
            return jnp.concatenate([sides[0 if b % CB == 0 else 1] for b in edges], axis=0)

        def edge(*spot):
            return jnp.concatenate(
                [
                    ref[(*lead, pl.ds(e * levels + index * chunk, chunk), slice(None))]
                    for ref, *lead in [spot]
                    for e in range(len(edges))
                ],
                axis=0,
            )

        chunk_keys, chunk_floor = take(keys, 2), take(floor, 2)
        product = edge(query_e) * per_edge(chunk_keys)
        squares = chunk_keys * chunk_keys
        scores = [jnp.sum(head(product, h, size), axis=-1, keepdims=True) for h in heads]
        means = [jnp.mean(head(squares, h, size), axis=-1, keepdims=True) for h in heads]
        norms = [per_edge(lax.rsqrt(m + chunk_floor)) for m in means]
        expons = [jnp.exp2(x * n) for x, n in zip(scores, norms)]
        den = edge(den_e)
        shares = [e / (den[:, h * size : h * size + 1] + e) for h, e in enumerate(expons)]
        result = edge(base_e)
        for h, share in enumerate(shares):
            result = result + share * (per_edge(take(moved[h], 2)) - edge(term_e, h))
        result = result.astype(BF)
        for e, b in enumerate(edges):
            there = pl.ds(b * levels + index * chunk, chunk)
            result_s[there, :] = result[e * chunk : (e + 1) * chunk]

    copy = pltpu.make_async_copy(result_s, out_ref, sem)
    copy.start()
    copy.wait()


def on_device(state, wet, w_vqkv, w_vout, w_hqkv, w_hout):
    tiles = lax.axis_size("tile")
    blocks, levels, width = state.shape
    rows = blocks // CB
    edge_rows = 2 * rows * levels
    limit = (10 << 20) + levels * (256 << 10)
    vmem = pl.BlockSpec(memory_space=pltpu.VMEM)
    hbm = pl.BlockSpec(memory_space=pl.ANY)
    whole = jax.ShapeDtypeStruct((blocks * levels, width), BF)
    strip = state.reshape(rows, CB, levels, width)
    one = jax.ShapeDtypeStruct((levels, width), BF)
    to_right, to_left = pl.pallas_call(
        edge_kernel,
        out_shape=(one, one),
        in_specs=[hbm] * 2,
        out_specs=(vmem,) * 2,
        scratch_shapes=[
            pltpu.SMEM((1, wet.shape[0]), wet.dtype),
            pltpu.VMEM((2, rows, levels, width), BF),
            pltpu.SemaphoreType.DMA((3,)),
        ],
        compiler_params=pltpu.CompilerParams(vmem_limit_bytes=4 << 20),
        cost_estimate=pl.CostEstimate(flops=200 << 30, bytes_accessed=1 << 30, transcendentals=0),
        name="edge_blocks",
    )(*[pltpu.with_memory_space_constraint(v, pltpu.HBM) for v in (wet.reshape(1, -1), strip)])
    from_left = lax.ppermute(to_right, "tile", [(i, (i + 1) % tiles) for i in range(tiles)])
    edge_f32 = jax.ShapeDtypeStruct((edge_rows, width), F32)
    results = (
        whole,
        edge_f32,
        edge_f32,
        jax.ShapeDtypeStruct((HEADS, edge_rows, width), F32),
        edge_f32,
    )
    operands = (
        state.reshape(blocks * levels, width), w_vqkv, w_vout, wet.reshape(1, -1), w_hqkv, w_hout
    )
    mixed_s = pltpu.VMEM((blocks * levels, width), BF)
    cost = pl.CostEstimate(
        flops=2 * blocks * levels * width * width * 8, bytes_accessed=8 << 20, transcendentals=0
    )
    *early, to_left = pl.pallas_call(
        functools.partial(early_kernel, levels),
        out_shape=results + (jax.ShapeDtypeStruct(to_left.shape, to_left.dtype),),
        in_specs=[hbm] * 6 + [vmem],
        out_specs=(vmem,) * 6,
        compiler_params=pltpu.CompilerParams(vmem_limit_bytes=limit + (6 << 20)),
        cost_estimate=cost,
        name="early_blocks",
    )(*[pltpu.with_memory_space_constraint(v, pltpu.HBM) for v in operands], to_left)
    from_right = lax.ppermute(to_left, "tile", [(i, (i - 1) % tiles) for i in range(tiles)])

    inner, *edge_values = pl.pallas_call(
        functools.partial(late_kernel, levels),
        out_shape=results,
        in_specs=[vmem] * 11,
        out_specs=(vmem,) * 5,
        scratch_shapes=[mixed_s],
        compiler_params=pltpu.CompilerParams(vmem_limit_bytes=limit),
        cost_estimate=cost,
        name="late_blocks",
    )(*operands, *early)
    updated = pl.pallas_call(
        functools.partial(halo_kernel, levels, blocks),
        out_shape=whole,
        in_specs=[vmem] * 11,
        out_specs=hbm,
        scratch_shapes=[
            pltpu.VMEM(whole.shape, BF),
            pltpu.SemaphoreType.DMA,
        ],
        compiler_params=pltpu.CompilerParams(vmem_limit_bytes=limit),
        name="halo_blocks",
    )(from_left, from_right, *edge_values, w_vqkv, w_vout, w_hqkv, w_hout, inner)
    return updated.reshape(blocks, levels, width)


def solution(mesh):
    in_specs = (P(("grp", "tile"), None, None), P(), P(), P(), P(), P())
    out_specs = P(("grp", "tile"), None, None)
    return jax.shard_map(
        on_device, mesh=mesh, in_specs=in_specs, out_specs=out_specs, check_vma=False
    )
```

```python
import functools
import math

import jax
import jax.numpy as jnp
from jax import lax
from jax.experimental import pallas as pl
from jax.experimental.pallas import tpu as pltpu
from jax.sharding import PartitionSpec as P

HEADS = 4
CB = 4
EPSILON = 1e-06
BF = jnp.bfloat16
F32 = jnp.float32


def each(count, body):
    if count == 1:
        body(0)
    else:
        pl.loop(0, count)(body)


def rows_at(start, size):
    if isinstance(start, int):
        return pl.ds(start, size)
    return pl.ds(pl.multiple_of(start, size), size)


def dot(left, right):
    return jnp.dot(left, right, preferred_element_type=F32)


def dot_t(left, right):
    return lax.dot_general(left, right, (((1,), (1,)), ((), ())), preferred_element_type=F32)


def head(values, index, size):
    return values[:, index * size : (index + 1) * size]


def with_ones(values):
    return jnp.concatenate([values, jnp.ones(values.shape, values.dtype)], axis=1)


def mean_square(values):
    return jnp.mean(values * values, axis=-1, keepdims=True) + EPSILON


def same_block(rows, levels):
    row = lax.broadcasted_iota(jnp.int32, (rows, rows), 0) // levels
    col = lax.broadcasted_iota(jnp.int32, (rows, rows), 1) // levels
    return row == col


def rms_normed(values):
    mean = jnp.mean(values * values, axis=-1, keepdims=True)
    return (values * lax.rsqrt(mean + EPSILON)).astype(BF)


def normed_heads(joined, size):
    return [rms_normed(head(joined, h, size)) for h in range(HEADS)]


def attention(queries, keys, values, allowed):
    size = queries[0].shape[1]
    scale = math.log2(math.e) / math.sqrt(size)
    scores = [dot_t(q, k) for q, k in zip(queries, keys)]
    expons = [jnp.exp2(x * scale) for x in scores]
    if allowed is not None:
        expons = [jnp.where(allowed, e, 0.0) for e in expons]
    totals = [jnp.sum(e, axis=-1, keepdims=True) for e in expons]
    probs = [(e / t).astype(BF) for e, t in zip(expons, totals)]
    contexts = [dot(p, head(values, h, size)).astype(BF) for h, p in enumerate(probs)]
    return contexts, totals


def vertical_context(block, w_vqkv, levels):
    rows, width = block.shape
    size = width // HEADS
    normed = rms_normed(block.astype(F32))
    keys = normed_heads(dot(normed, w_vqkv[:, width : 2 * width]), size)
    queries = normed_heads(dot(normed, w_vqkv[:, :width]), size)
    values = dot(normed, w_vqkv[:, 2 * width :]).astype(BF)
    allowed = same_block(rows, levels) if rows > levels else None
    return jnp.concatenate(attention(queries, keys, values, allowed)[0], axis=1)


def halo_context(block, w_vqkv, levels):
    rows, width = block.shape
    size = width // HEADS
    scale = math.log2(math.e) / math.sqrt(size)
    values = block.astype(F32)
    heads = range(HEADS)
    keys = dot(block, w_vqkv[:, width : 2 * width])
    queries = dot(block, w_vqkv[:, :width])
    vals = dot(block, w_vqkv[:, 2 * width :])
    squares = mean_square(values)
    squares_k = dot_t(jnp.full((8, width), 1.0 / width, BF), (values * values).astype(BF))[0:1]
    floor, floor_k = squares * EPSILON, (squares_k + EPSILON) * EPSILON
    keys_sq = (keys * keys).astype(BF)
    queries_b, keys_b = queries.astype(BF), keys.astype(BF)
    scores = [dot_t(head(queries_b, h, size), head(keys_b, h, size)) for h in heads]
    ones = jnp.full((8, size), 1.0 / size, BF)
    means_k = [dot_t(ones, head(keys_sq, h, size))[0:1] for h in heads]
    norms_q = [
        lax.rsqrt(jnp.mean(q * q, axis=-1, keepdims=True) + floor) * scale
        for q in (head(queries, h, size) for h in heads)
    ]
    norms_k = [lax.rsqrt(m + floor_k) for m in means_k]
    vals = (vals * lax.rsqrt(squares)).astype(BF)
    expons = [jnp.exp2(x * q * k) for x, q, k in zip(scores, norms_q, norms_k)]
    if rows > levels:
        inside = same_block(rows, levels)
        expons = [jnp.where(inside, e, 0.0) for e in expons]
    totals = [dot(e.astype(BF), with_ones(head(vals, h, size))) for h, e in enumerate(expons)]
    parts = [(t[:, :size] / t[:, size:]).astype(BF) for t in totals]
    return jnp.concatenate(parts, axis=1)


def edge_kernel(wet_hbm, x_hbm, to_right, to_left, wet_ref, held, sems):
    blocks = x_hbm.shape[0] * CB
    tile = lax.axis_index("tile")
    copies = [
        pltpu.make_async_copy(wet_hbm, wet_ref, sems.at[0]),
        pltpu.make_async_copy(x_hbm.at[:, CB - 1], held.at[0], sems.at[1]),
        pltpu.make_async_copy(x_hbm.at[:, 0], held.at[1], sems.at[2]),
    ]
    for copy in copies:
        copy.start()
    for copy in copies:
        copy.wait()
    for i, (out_ref, column) in enumerate(((to_right, CB - 1), (to_left, 0))):
        out_ref[...] = jnp.where(wet_ref[0, tile * blocks + column] > 0, held[i, 0], held[i, 1])


def early_kernel(levels, *refs):
    operands, outputs = refs[:6], refs[7:12]
    refs[12][...] = refs[6][...]

    def run(*scratch):
        *loaded, mixed_s, sems = scratch
        copies = [
            pltpu.make_async_copy(a, b, sems.at[i]) for i, (a, b) in enumerate(zip(operands, loaded))
        ]
        for copy in copies:
            copy.start()
        own_blocks(levels, *loaded, *outputs, mixed_s, copies)

    @pl.when(lax.axis_index("tile") == 0)
    def _():
        pl.run_scoped(
            run,
            *[pltpu.VMEM(ref.shape, ref.dtype) for ref in operands],
            pltpu.VMEM(operands[0].shape, BF),
            pltpu.SemaphoreType.DMA((len(operands),)),
        )


def late_kernel(levels, *refs):
    operands, early, outputs, mixed_s = refs[:6], refs[6:11], refs[11:16], refs[16]

    @pl.when(lax.axis_index("tile") == 0)
    def _():
        for source, target in zip(early, outputs):
            target[...] = source[...]

    @pl.when(lax.axis_index("tile") != 0)
    def _():
        own_blocks(levels, *operands, *outputs, mixed_s, ())


def own_blocks(
    levels, x_ref, w_vqkv, w_vout, wet_ref, w_hqkv, w_hout,
    result_ref, base_e, query_e, term_e, den_e, mixed_s, copies,
):
    total_rows, width = x_ref.shape
    size = width // HEADS
    blocks = total_rows // levels
    chunk = min(levels, 16)
    edges = [b for b in range(blocks) if b % CB in (0, CB - 1)]
    tile = lax.axis_index("tile")
    group = min(max(levels, 128), total_rows)

    def mix(index):
        rows = rows_at(index * group, group)
        block = x_ref[rows, :]
        context = vertical_context(block, w_vqkv, levels)
        mixed_s[rows, :] = (block.astype(F32) + dot(context, w_vout[...])).astype(BF)

    for copy in copies[:3]:
        copy.wait()
    each(total_rows // group, mix)
    for copy in copies[3:]:
        copy.wait()

    rows = blocks * chunk
    row = lax.broadcasted_iota(jnp.int32, (rows, rows), 0)
    col = lax.broadcasted_iota(jnp.int32, (rows, rows), 1)
    block_q, block_k = row // chunk, col // chunk
    wet = jnp.broadcast_to(wet_ref[...], (8, wet_ref.shape[1])).astype(BF)
    which = lax.broadcasted_iota(jnp.int32, (wet.shape[1], rows), 0)
    column = lax.broadcasted_iota(jnp.int32, (wet.shape[1], rows), 1) // chunk
    wet_k = dot(wet, (which == tile * blocks + column).astype(BF))[0:1, :]
    near = jnp.abs(block_q % CB - block_k % CB) <= 1
    near = near & (jnp.abs(block_q // CB - block_k // CB) <= 1)
    allowed = (row % chunk == col % chunk) & ((block_q == block_k) | (near & (wet_k > 0.5)))

    def attend(index):
        def spots(b):
            return rows_at(b * levels + index * chunk, chunk)

        mixed = jnp.concatenate([mixed_s[spots(b), :] for b in range(blocks)], axis=0)
        values = mixed.astype(F32)
        joined = dot(rms_normed(values), w_hqkv[...])
        queries = normed_heads(joined[:, :width], size)
        keys = normed_heads(joined[:, width : 2 * width], size)
        parts, totals = attention(queries, keys, joined[:, 2 * width :].astype(BF), allowed)
        inner = [b for b in range(blocks) if b not in edges]

        def some(array, which):
            return jnp.concatenate([array[b * chunk : (b + 1) * chunk] for b in which], axis=0)

        context = jnp.concatenate([some(p, inner) for p in parts], axis=1)
        result = (some(values, inner) + dot(context, w_hout[...])).astype(BF)
        terms = [
            dot(some(p, edges), w_hout[h * size : (h + 1) * size, :]) for h, p in enumerate(parts)
        ]
        base = some(values, edges) + sum(terms)
        for i, b in enumerate(inner):
            result_ref[spots(b), :] = result[i * chunk : (i + 1) * chunk]
        for e, b in enumerate(edges):
            here = slice(e * chunk, (e + 1) * chunk)
            there = rows_at(e * levels + index * chunk, chunk)
            base_e[there, :] = base[here]
            for h in range(HEADS):
                cols = slice(h * size, (h + 1) * size)
                query_e[there, cols] = queries[h][b * chunk : (b + 1) * chunk].astype(F32)
                den_e[there, cols] = jnp.broadcast_to(
                    totals[h][b * chunk : (b + 1) * chunk], (chunk, size)
                )
                term_e[h, there, :] = terms[h][here]

    each(levels // chunk, attend)


def halo_kernel(
    levels, blocks, from_left, from_right, base_e, query_e, term_e, den_e,
    w_vqkv, w_vout, w_hqkv, w_hout, inner_ref, result_s,
):
    width = base_e.shape[1]
    size = width // HEADS
    scale = math.log2(math.e) / math.sqrt(size)
    chunk = min(levels, 16)
    edges = [b for b in range(blocks) if b % CB in (0, CB - 1)]
    group = 2 * levels if 2 * levels <= 128 else levels
    for b in range(blocks):
        if b not in edges:
            here = pl.ds(b * levels, levels)
            result_s[here, :] = inner_ref[here, :]

    halo = jnp.concatenate([from_left[...], from_right[...]], axis=0)
    heads = range(HEADS)
    pieces = []
    for start in range(0, 2 * levels, group):
        block = halo[start : start + group]
        context = halo_context(block, w_vqkv, levels)
        mixed = (block.astype(F32) + dot(context, w_vout[...])).astype(BF)
        joined = dot(mixed, w_hqkv[:, width:])
        mixed = mixed.astype(F32)
        squares = mean_square(mixed)
        values = (joined[:, width:] * lax.rsqrt(squares)).astype(BF)
        moved = []
        empty = jnp.zeros((group, size), BF)
        for h in range(0, HEADS, 2):
            one, two = head(values, h, size), head(values, h + 1, size)
            both = jnp.concatenate(
                [jnp.concatenate([one, empty], axis=1), jnp.concatenate([empty, two], axis=1)], axis=0
            )
            total = dot(both, w_hout[h * size : (h + 2) * size, :])
            moved += [total[:group], total[group:]]
        pieces.append((joined[:, :width], squares * EPSILON, *moved))
    keys, floor, *moved = (jnp.concatenate(p, axis=0) for p in zip(*pieces))

    for index in range(levels // chunk):
        def take(source, count):
            return jnp.concatenate(
                [source[i * levels + index * chunk :][:chunk] for i in range(count)], axis=0
            )

        def per_edge(values):
            sides = [values[:chunk], values[chunk:]]
            return jnp.concatenate([sides[0 if b % CB == 0 else 1] for b in edges], axis=0)

        def edge(*spot):
            return jnp.concatenate(
                [
                    ref[(*lead, pl.ds(e * levels + index * chunk, chunk), slice(None))]
                    for ref, *lead in [spot]
                    for e in range(len(edges))
                ],
                axis=0,
            )

        chunk_keys, chunk_floor = take(keys, 2), take(floor, 2)
        product = edge(query_e) * per_edge(chunk_keys)
        squares = chunk_keys * chunk_keys
        scores = [jnp.sum(head(product, h, size), axis=-1, keepdims=True) for h in heads]
        means = [jnp.mean(head(squares, h, size), axis=-1, keepdims=True) for h in heads]
        norms = [per_edge(lax.rsqrt(m + chunk_floor) * scale) for m in means]
        den = edge(den_e)
        shares = [
            1.0 / (1.0 + den[:, h * size : h * size + 1] * jnp.exp2(-(x * n)))
            for h, (x, n) in enumerate(zip(scores, norms))
        ]
        result = edge(base_e)
        for h, share in enumerate(shares):
            result = result + share * (per_edge(take(moved[h], 2)) - edge(term_e, h))
        result = result.astype(BF)
        for e, b in enumerate(edges):
            there = pl.ds(b * levels + index * chunk, chunk)
            result_s[there, :] = result[e * chunk : (e + 1) * chunk]


def on_device(state, wet, w_vqkv, w_vout, w_hqkv, w_hout):
    tiles = lax.axis_size("tile")
    blocks, levels, width = state.shape
    rows = blocks // CB
    edge_rows = 2 * rows * levels
    limit = (10 << 20) + levels * (256 << 10)
    vmem = pl.BlockSpec(memory_space=pltpu.VMEM)
    hbm = pl.BlockSpec(memory_space=pl.ANY)
    whole = jax.ShapeDtypeStruct((blocks * levels, width), BF)
    strip = state.reshape(rows, CB, levels, width)
    one = jax.ShapeDtypeStruct((levels, width), BF)
    to_right, to_left = pl.pallas_call(
        edge_kernel,
        out_shape=(one, one),
        in_specs=[hbm] * 2,
        out_specs=(vmem,) * 2,
        scratch_shapes=[
            pltpu.SMEM((1, wet.shape[0]), wet.dtype),
            pltpu.VMEM((2, rows, levels, width), BF),
            pltpu.SemaphoreType.DMA((3,)),
        ],
        compiler_params=pltpu.CompilerParams(vmem_limit_bytes=4 << 20),
        cost_estimate=pl.CostEstimate(flops=200 << 30, bytes_accessed=1 << 30, transcendentals=0),
        name="edge_blocks",
    )(*[pltpu.with_memory_space_constraint(v, pltpu.HBM) for v in (wet.reshape(1, -1), strip)])
    from_left = lax.ppermute(to_right, "tile", [(i, (i + 1) % tiles) for i in range(tiles)])
    edge_f32 = jax.ShapeDtypeStruct((edge_rows, width), F32)
    results = (
        whole,
        edge_f32,
        edge_f32,
        jax.ShapeDtypeStruct((HEADS, edge_rows, width), F32),
        edge_f32,
    )
    operands = (
        state.reshape(blocks * levels, width), w_vqkv, w_vout, wet.reshape(1, -1), w_hqkv, w_hout
    )
    mixed_s = pltpu.VMEM((blocks * levels, width), BF)
    cost = pl.CostEstimate(
        flops=2 * blocks * levels * width * width * 8, bytes_accessed=8 << 20, transcendentals=0
    )
    *early, to_left = pl.pallas_call(
        functools.partial(early_kernel, levels),
        out_shape=results + (jax.ShapeDtypeStruct(to_left.shape, to_left.dtype),),
        in_specs=[hbm] * 6 + [vmem],
        out_specs=(vmem,) * 6,
        compiler_params=pltpu.CompilerParams(vmem_limit_bytes=limit + (6 << 20)),
        cost_estimate=cost,
        name="early_blocks",
    )(*[pltpu.with_memory_space_constraint(v, pltpu.HBM) for v in operands], to_left)
    from_right = lax.ppermute(to_left, "tile", [(i, (i - 1) % tiles) for i in range(tiles)])

    inner, *edge_values = pl.pallas_call(
        functools.partial(late_kernel, levels),
        out_shape=results,
        in_specs=[vmem] * 11,
        out_specs=(vmem,) * 5,
        scratch_shapes=[mixed_s],
        compiler_params=pltpu.CompilerParams(vmem_limit_bytes=limit),
        cost_estimate=cost,
        name="late_blocks",
    )(*operands, *early)
    updated = pl.pallas_call(
        functools.partial(halo_kernel, levels, blocks),
        out_shape=whole,
        in_specs=[vmem] * 11,
        out_specs=vmem,
        compiler_params=pltpu.CompilerParams(vmem_limit_bytes=limit),
        name="halo_blocks",
    )(from_left, from_right, *edge_values, w_vqkv, w_vout, w_hqkv, w_hout, inner)
    return updated.reshape(blocks, levels, width)


def solution(mesh):
    in_specs = (P(("grp", "tile"), None, None), P(), P(), P(), P(), P())
    out_specs = P(("grp", "tile"), None, None)
    return jax.shard_map(
        on_device, mesh=mesh, in_specs=in_specs, out_specs=out_specs, check_vma=False
    )
```

```python
import functools
import math

import jax
import jax.numpy as jnp
from jax import lax
from jax.experimental import pallas as pl
from jax.experimental.pallas import tpu as pltpu
from jax.sharding import PartitionSpec as P

HEADS = 4
CB = 4
EPSILON = 1e-06
BF = jnp.bfloat16
F32 = jnp.float32


def each(count, body):
    if count == 1:
        body(0)
    else:
        pl.loop(0, count)(body)


def rows_at(start, size):
    if isinstance(start, int):
        return pl.ds(start, size)
    return pl.ds(pl.multiple_of(start, size), size)


def dot(left, right):
    return jnp.dot(left, right, preferred_element_type=F32)


def dot_t(left, right):
    return lax.dot_general(left, right, (((1,), (1,)), ((), ())), preferred_element_type=F32)


def head(values, index, size):
    return values[:, index * size : (index + 1) * size]


def with_ones(values):
    return jnp.concatenate([values, jnp.ones(values.shape, values.dtype)], axis=1)


def mean_square(values):
    return jnp.mean(values * values, axis=-1, keepdims=True) + EPSILON


def same_block(rows, levels):
    row = lax.broadcasted_iota(jnp.int32, (rows, rows), 0) // levels
    col = lax.broadcasted_iota(jnp.int32, (rows, rows), 1) // levels
    return row == col


def rms_normed(values):
    mean = jnp.mean(values * values, axis=-1, keepdims=True)
    return (values * lax.rsqrt(mean + EPSILON)).astype(BF)


def normed_heads(joined, size):
    return [rms_normed(head(joined, h, size)) for h in range(HEADS)]


def attention(queries, keys, values, allowed):
    size = queries[0].shape[1]
    scale = math.log2(math.e) / math.sqrt(size)
    scores = [dot_t(q, k) for q, k in zip(queries, keys)]
    expons = [jnp.exp2(x * scale) for x in scores]
    if allowed is not None:
        expons = [jnp.where(allowed, e, 0.0) for e in expons]
    totals = [jnp.sum(e, axis=-1, keepdims=True) for e in expons]
    probs = [(e / t).astype(BF) for e, t in zip(expons, totals)]
    contexts = [dot(p, head(values, h, size)).astype(BF) for h, p in enumerate(probs)]
    return contexts, totals


def vertical_context(block, w_vqkv, levels):
    rows, width = block.shape
    size = width // HEADS
    normed = rms_normed(block.astype(F32))
    keys = normed_heads(dot(normed, w_vqkv[:, width : 2 * width]), size)
    queries = normed_heads(dot(normed, w_vqkv[:, :width]), size)
    values = dot(normed, w_vqkv[:, 2 * width :]).astype(BF)
    allowed = same_block(rows, levels) if rows > levels else None
    return jnp.concatenate(attention(queries, keys, values, allowed)[0], axis=1)


def halo_context(block, w_vqkv, levels):
    rows, width = block.shape
    size = width // HEADS
    scale = math.log2(math.e) / math.sqrt(size)
    values = block.astype(F32)
    heads = range(HEADS)
    keys = dot(block, w_vqkv[:, width : 2 * width])
    queries = dot(block, w_vqkv[:, :width])
    vals = dot(block, w_vqkv[:, 2 * width :])
    squares = mean_square(values)
    squares_k = dot_t(jnp.full((8, width), 1.0 / width, BF), (values * values).astype(BF))[0:1]
    floor, floor_k = squares * EPSILON, (squares_k + EPSILON) * EPSILON
    keys_sq = (keys * keys).astype(BF)
    queries_b, keys_b = queries.astype(BF), keys.astype(BF)
    scores = [dot_t(head(queries_b, h, size), head(keys_b, h, size)) for h in heads]
    ones = jnp.full((8, size), 1.0 / size, BF)
    means_k = [dot_t(ones, head(keys_sq, h, size))[0:1] for h in heads]
    norms_q = [
        lax.rsqrt(jnp.mean(q * q, axis=-1, keepdims=True) + floor) * scale
        for q in (head(queries, h, size) for h in heads)
    ]
    norms_k = [lax.rsqrt(m + floor_k) for m in means_k]
    vals = (vals * lax.rsqrt(squares)).astype(BF)
    expons = [jnp.exp2(x * q * k) for x, q, k in zip(scores, norms_q, norms_k)]
    if rows > levels:
        inside = same_block(rows, levels)
        expons = [jnp.where(inside, e, 0.0) for e in expons]
    totals = [dot(e.astype(BF), with_ones(head(vals, h, size))) for h, e in enumerate(expons)]
    parts = [(t[:, :size] / t[:, size:]).astype(BF) for t in totals]
    return jnp.concatenate(parts, axis=1)


def edge_kernel(wet_hbm, x_hbm, to_right, to_left, wet_ref, held, sems):
    blocks = x_hbm.shape[0] * CB
    tile = lax.axis_index("tile")
    copies = [
        pltpu.make_async_copy(wet_hbm, wet_ref, sems.at[0]),
        pltpu.make_async_copy(x_hbm.at[:, CB - 1], held.at[0], sems.at[1]),
        pltpu.make_async_copy(x_hbm.at[:, 0], held.at[1], sems.at[2]),
    ]
    for copy in copies:
        copy.start()
    for copy in copies:
        copy.wait()
    for i, (out_ref, column) in enumerate(((to_right, CB - 1), (to_left, 0))):
        out_ref[...] = jnp.where(wet_ref[0, tile * blocks + column] > 0, held[i, 0], held[i, 1])


def early_kernel(levels, *refs):
    operands, outputs = refs[:6], refs[7:12]
    refs[12][...] = refs[6][...]

    def run(*scratch):
        *loaded, mixed_s, sems = scratch
        copies = [
            pltpu.make_async_copy(a, b, sems.at[i]) for i, (a, b) in enumerate(zip(operands, loaded))
        ]
        for copy in copies:
            copy.start()
        for copy in copies[:3]:
            copy.wait()
        own_vertical(levels, *loaded[:3], mixed_s)
        for copy in copies[3:]:
            copy.wait()
        own_horizontal(levels, mixed_s, *loaded[3:], *outputs)

    @pl.when(lax.axis_index("tile") == 0)
    def _():
        pl.run_scoped(
            run,
            *[pltpu.VMEM(ref.shape, ref.dtype) for ref in operands],
            pltpu.VMEM(operands[0].shape, BF),
            pltpu.SemaphoreType.DMA((len(operands),)),
        )


def vertical_kernel(levels, x_ref, w_vqkv, w_vout, mixed_ref):
    @pl.when(lax.axis_index("tile") != 0)
    def _():
        own_vertical(levels, x_ref, w_vqkv, w_vout, mixed_ref)


def horizontal_kernel(levels, *refs):
    operands, early, outputs = refs[:4], refs[4:9], refs[9:]

    @pl.when(lax.axis_index("tile") == 0)
    def _():
        for source, target in zip(early, outputs):
            target[...] = source[...]

    @pl.when(lax.axis_index("tile") != 0)
    def _():
        own_horizontal(levels, *operands, *outputs)


def own_vertical(levels, x_ref, w_vqkv, w_vout, mixed_ref):
    total_rows = x_ref.shape[0]
    group = min(max(levels, 128), total_rows)

    def mix(index):
        rows = rows_at(index * group, group)
        block = x_ref[rows, :]
        context = vertical_context(block, w_vqkv, levels)
        mixed_ref[rows, :] = (block.astype(F32) + dot(context, w_vout[...])).astype(BF)

    each(total_rows // group, mix)


def own_horizontal(
    levels, mixed_ref, wet_ref, w_hqkv, w_hout, result_ref, base_e, query_e, term_e, den_e
):
    total_rows, width = mixed_ref.shape
    size = width // HEADS
    blocks = total_rows // levels
    chunk = min(levels, 16)
    edges = [b for b in range(blocks) if b % CB in (0, CB - 1)]
    tile = lax.axis_index("tile")

    rows = blocks * chunk
    row = lax.broadcasted_iota(jnp.int32, (rows, rows), 0)
    col = lax.broadcasted_iota(jnp.int32, (rows, rows), 1)
    block_q, block_k = row // chunk, col // chunk
    wet = jnp.broadcast_to(wet_ref[...], (8, wet_ref.shape[1])).astype(BF)
    which = lax.broadcasted_iota(jnp.int32, (wet.shape[1], rows), 0)
    column = lax.broadcasted_iota(jnp.int32, (wet.shape[1], rows), 1) // chunk
    wet_k = dot(wet, (which == tile * blocks + column).astype(BF))[0:1, :]
    near = jnp.abs(block_q % CB - block_k % CB) <= 1
    near = near & (jnp.abs(block_q // CB - block_k // CB) <= 1)
    allowed = (row % chunk == col % chunk) & ((block_q == block_k) | (near & (wet_k > 0.5)))

    def attend(index):
        def spots(b):
            return rows_at(b * levels + index * chunk, chunk)

        mixed = jnp.concatenate([mixed_ref[spots(b), :] for b in range(blocks)], axis=0)
        values = mixed.astype(F32)
        joined = dot(rms_normed(values), w_hqkv[...])
        queries = normed_heads(joined[:, :width], size)
        keys = normed_heads(joined[:, width : 2 * width], size)
        parts, totals = attention(queries, keys, joined[:, 2 * width :].astype(BF), allowed)
        inner = [b for b in range(blocks) if b not in edges]

        def some(array, which):
            return jnp.concatenate([array[b * chunk : (b + 1) * chunk] for b in which], axis=0)

        context = jnp.concatenate([some(p, inner) for p in parts], axis=1)
        result = (some(values, inner) + dot(context, w_hout[...])).astype(BF)
        terms = [
            dot(some(p, edges), w_hout[h * size : (h + 1) * size, :]) for h, p in enumerate(parts)
        ]
        base = some(values, edges) + sum(terms)
        for i, b in enumerate(inner):
            result_ref[spots(b), :] = result[i * chunk : (i + 1) * chunk]
        for e, b in enumerate(edges):
            here = slice(e * chunk, (e + 1) * chunk)
            there = rows_at(e * levels + index * chunk, chunk)
            base_e[there, :] = base[here]
            for h in range(HEADS):
                cols = slice(h * size, (h + 1) * size)
                query_e[there, cols] = queries[h][b * chunk : (b + 1) * chunk].astype(F32)
                den_e[there, cols] = jnp.broadcast_to(
                    totals[h][b * chunk : (b + 1) * chunk], (chunk, size)
                )
                term_e[h, there, :] = terms[h][here]

    each(levels // chunk, attend)


def halo_kernel(
    levels, blocks, from_left, from_right, base_e, query_e, term_e, den_e,
    w_vqkv, w_vout, w_hqkv, w_hout, inner_ref, result_s,
):
    width = base_e.shape[1]
    size = width // HEADS
    scale = math.log2(math.e) / math.sqrt(size)
    chunk = min(levels, 16)
    edges = [b for b in range(blocks) if b % CB in (0, CB - 1)]
    group = 2 * levels if 2 * levels <= 128 else levels
    for b in range(blocks):
        if b not in edges:
            here = pl.ds(b * levels, levels)
            result_s[here, :] = inner_ref[here, :]

    halo = jnp.concatenate([from_left[...], from_right[...]], axis=0)
    heads = range(HEADS)
    pieces = []
    for start in range(0, 2 * levels, group):
        block = halo[start : start + group]
        context = halo_context(block, w_vqkv, levels)
        mixed = (block.astype(F32) + dot(context, w_vout[...])).astype(BF)
        joined = dot(mixed, w_hqkv[:, width:])
        mixed = mixed.astype(F32)
        squares = mean_square(mixed)
        values = (joined[:, width:] * lax.rsqrt(squares)).astype(BF)
        moved = []
        empty = jnp.zeros((group, size), BF)
        for h in range(0, HEADS, 2):
            one, two = head(values, h, size), head(values, h + 1, size)
            both = jnp.concatenate(
                [jnp.concatenate([one, empty], axis=1), jnp.concatenate([empty, two], axis=1)], axis=0
            )
            total = dot(both, w_hout[h * size : (h + 2) * size, :])
            moved += [total[:group], total[group:]]
        pieces.append((joined[:, :width], squares * EPSILON, *moved))
    keys, floor, *moved = (jnp.concatenate(p, axis=0) for p in zip(*pieces))

    for index in range(levels // chunk):
        def take(source, count):
            return jnp.concatenate(
                [source[i * levels + index * chunk :][:chunk] for i in range(count)], axis=0
            )

        def per_edge(values):
            sides = [values[:chunk], values[chunk:]]
            return jnp.concatenate([sides[0 if b % CB == 0 else 1] for b in edges], axis=0)

        def edge(*spot):
            return jnp.concatenate(
                [
                    ref[(*lead, pl.ds(e * levels + index * chunk, chunk), slice(None))]
                    for ref, *lead in [spot]
                    for e in range(len(edges))
                ],
                axis=0,
            )

        chunk_keys, chunk_floor = take(keys, 2), take(floor, 2)
        product = edge(query_e) * per_edge(chunk_keys)
        squares = chunk_keys * chunk_keys
        scores = [jnp.sum(head(product, h, size), axis=-1, keepdims=True) for h in heads]
        means = [jnp.mean(head(squares, h, size), axis=-1, keepdims=True) for h in heads]
        norms = [per_edge(lax.rsqrt(m + chunk_floor) * scale) for m in means]
        den = edge(den_e)
        shares = [
            1.0 / (1.0 + den[:, h * size : h * size + 1] * jnp.exp2(-(x * n)))
            for h, (x, n) in enumerate(zip(scores, norms))
        ]
        result = edge(base_e)
        for h, share in enumerate(shares):
            result = result + share * (per_edge(take(moved[h], 2)) - edge(term_e, h))
        result = result.astype(BF)
        for e, b in enumerate(edges):
            there = pl.ds(b * levels + index * chunk, chunk)
            result_s[there, :] = result[e * chunk : (e + 1) * chunk]


def on_device(state, wet, w_vqkv, w_vout, w_hqkv, w_hout):
    tiles = lax.axis_size("tile")
    blocks, levels, width = state.shape
    rows = blocks // CB
    edge_rows = 2 * rows * levels
    limit = (10 << 20) + levels * (256 << 10)
    vmem = pl.BlockSpec(memory_space=pltpu.VMEM)
    hbm = pl.BlockSpec(memory_space=pl.ANY)
    whole = jax.ShapeDtypeStruct((blocks * levels, width), BF)
    strip = state.reshape(rows, CB, levels, width)
    one = jax.ShapeDtypeStruct((levels, width), BF)
    to_right, to_left = pl.pallas_call(
        edge_kernel,
        out_shape=(one, one),
        in_specs=[hbm] * 2,
        out_specs=(vmem,) * 2,
        scratch_shapes=[
            pltpu.SMEM((1, wet.shape[0]), wet.dtype),
            pltpu.VMEM((2, rows, levels, width), BF),
            pltpu.SemaphoreType.DMA((3,)),
        ],
        compiler_params=pltpu.CompilerParams(vmem_limit_bytes=4 << 20),
        cost_estimate=pl.CostEstimate(flops=200 << 30, bytes_accessed=1 << 30, transcendentals=0),
        name="edge_blocks",
    )(*[pltpu.with_memory_space_constraint(v, pltpu.HBM) for v in (wet.reshape(1, -1), strip)])
    from_left = lax.ppermute(to_right, "tile", [(i, (i + 1) % tiles) for i in range(tiles)])
    edge_f32 = jax.ShapeDtypeStruct((edge_rows, width), F32)
    results = (
        whole,
        edge_f32,
        edge_f32,
        jax.ShapeDtypeStruct((HEADS, edge_rows, width), F32),
        edge_f32,
    )
    operands = (
        state.reshape(blocks * levels, width), w_vqkv, w_vout, wet.reshape(1, -1), w_hqkv, w_hout
    )
    work = blocks * levels * width * width
    cost = pl.CostEstimate(flops=8 * work, bytes_accessed=4 << 20, transcendentals=0)
    *early, to_left = pl.pallas_call(
        functools.partial(early_kernel, levels),
        out_shape=results + (jax.ShapeDtypeStruct(to_left.shape, to_left.dtype),),
        in_specs=[hbm] * 6 + [vmem],
        out_specs=(vmem,) * 6,
        compiler_params=pltpu.CompilerParams(vmem_limit_bytes=limit + (6 << 20)),
        cost_estimate=cost,
        name="early_blocks",
    )(*[pltpu.with_memory_space_constraint(v, pltpu.HBM) for v in operands], to_left)
    from_right = lax.ppermute(to_left, "tile", [(i, (i - 1) % tiles) for i in range(tiles)])

    mixed = pl.pallas_call(
        functools.partial(vertical_kernel, levels),
        out_shape=whole,
        in_specs=[vmem] * 3,
        out_specs=vmem,
        compiler_params=pltpu.CompilerParams(vmem_limit_bytes=limit),
        cost_estimate=cost,
        name="vertical_blocks",
    )(*operands[:3])
    inner, *edge_values = pl.pallas_call(
        functools.partial(horizontal_kernel, levels),
        out_shape=results,
        in_specs=[vmem] * 9,
        out_specs=(vmem,) * 5,
        compiler_params=pltpu.CompilerParams(vmem_limit_bytes=limit),
        cost_estimate=cost,
        name="horizontal_blocks",
    )(mixed, *operands[3:], *early)
    updated = pl.pallas_call(
        functools.partial(halo_kernel, levels, blocks),
        out_shape=whole,
        in_specs=[vmem] * 11,
        out_specs=vmem,
        compiler_params=pltpu.CompilerParams(vmem_limit_bytes=limit),
        name="halo_blocks",
    )(from_left, from_right, *edge_values, w_vqkv, w_vout, w_hqkv, w_hout, inner)
    return updated.reshape(blocks, levels, width)


def solution(mesh):
    in_specs = (P(("grp", "tile"), None, None), P(), P(), P(), P(), P())
    out_specs = P(("grp", "tile"), None, None)
    return jax.shard_map(
        on_device, mesh=mesh, in_specs=in_specs, out_specs=out_specs, check_vma=False
    )
```

```python
import functools
import math

import jax
import jax.numpy as jnp
from jax import lax
from jax.experimental import pallas as pl
from jax.experimental.pallas import tpu as pltpu
from jax.sharding import PartitionSpec as P

HEADS = 4
CB = 4
EPSILON = 1e-06
BF = jnp.bfloat16
F32 = jnp.float32


def each(count, body):
    if count == 1:
        body(0)
    else:
        pl.loop(0, count)(body)


def rows_at(start, size):
    if isinstance(start, int):
        return pl.ds(start, size)
    return pl.ds(pl.multiple_of(start, size), size)


def dot(left, right):
    return jnp.dot(left, right, preferred_element_type=F32)


def dot_t(left, right):
    return lax.dot_general(left, right, (((1,), (1,)), ((), ())), preferred_element_type=F32)


def head(values, index, size):
    return values[:, index * size : (index + 1) * size]


def with_ones(values):
    return jnp.concatenate([values, jnp.ones(values.shape, values.dtype)], axis=1)


def mean_square(values):
    return jnp.mean(values * values, axis=-1, keepdims=True) + EPSILON


def same_block(rows, levels):
    row = lax.broadcasted_iota(jnp.int32, (rows, rows), 0) // levels
    col = lax.broadcasted_iota(jnp.int32, (rows, rows), 1) // levels
    return row == col


def rms_normed(values):
    mean = jnp.mean(values * values, axis=-1, keepdims=True)
    return (values * lax.rsqrt(mean + EPSILON)).astype(BF)


def normed_heads(joined, size):
    return [rms_normed(head(joined, h, size)) for h in range(HEADS)]


def attention(queries, keys, values, allowed):
    size = queries[0].shape[1]
    scale = math.log2(math.e) / math.sqrt(size)
    scores = [dot_t(q, k) for q, k in zip(queries, keys)]
    expons = [jnp.exp2(x * scale) for x in scores]
    if allowed is not None:
        expons = [jnp.where(allowed, e, 0.0) for e in expons]
    totals = [jnp.sum(e, axis=-1, keepdims=True) for e in expons]
    probs = [(e / t).astype(BF) for e, t in zip(expons, totals)]
    contexts = [dot(p, head(values, h, size)).astype(BF) for h, p in enumerate(probs)]
    return contexts, totals


def vertical_context(block, w_vqkv, levels):
    rows, width = block.shape
    size = width // HEADS
    normed = rms_normed(block.astype(F32))
    keys = normed_heads(dot(normed, w_vqkv[:, width : 2 * width]), size)
    queries = normed_heads(dot(normed, w_vqkv[:, :width]), size)
    values = dot(normed, w_vqkv[:, 2 * width :]).astype(BF)
    allowed = same_block(rows, levels) if rows > levels else None
    return jnp.concatenate(attention(queries, keys, values, allowed)[0], axis=1)


def halo_context(block, w_vqkv, levels):
    rows, width = block.shape
    size = width // HEADS
    scale = math.log2(math.e) / math.sqrt(size)
    values = block.astype(F32)
    heads = range(HEADS)
    keys = dot(block, w_vqkv[:, width : 2 * width])
    queries = dot(block, w_vqkv[:, :width])
    vals = dot(block, w_vqkv[:, 2 * width :])
    squares = mean_square(values)
    squares_k = dot_t(jnp.full((8, width), 1.0 / width, BF), (values * values).astype(BF))[0:1]
    floor, floor_k = squares * EPSILON, (squares_k + EPSILON) * EPSILON
    keys_sq = (keys * keys).astype(BF)
    queries_b, keys_b = queries.astype(BF), keys.astype(BF)
    scores = [dot_t(head(queries_b, h, size), head(keys_b, h, size)) for h in heads]
    ones = jnp.full((8, size), 1.0 / size, BF)
    means_k = [dot_t(ones, head(keys_sq, h, size))[0:1] for h in heads]
    norms_q = [
        lax.rsqrt(jnp.mean(q * q, axis=-1, keepdims=True) + floor) * scale
        for q in (head(queries, h, size) for h in heads)
    ]
    norms_k = [lax.rsqrt(m + floor_k) for m in means_k]
    vals = (vals * lax.rsqrt(squares)).astype(BF)
    expons = [jnp.exp2(x * q * k) for x, q, k in zip(scores, norms_q, norms_k)]
    if rows > levels:
        inside = same_block(rows, levels)
        expons = [jnp.where(inside, e, 0.0) for e in expons]
    totals = [dot(e.astype(BF), with_ones(head(vals, h, size))) for h, e in enumerate(expons)]
    parts = [(t[:, :size] / t[:, size:]).astype(BF) for t in totals]
    return jnp.concatenate(parts, axis=1)


def edge_kernel(wet_hbm, x_hbm, to_right, to_left, wet_ref, held, sems):
    blocks = x_hbm.shape[0] * CB
    tile = lax.axis_index("tile")
    copies = [
        pltpu.make_async_copy(wet_hbm, wet_ref, sems.at[0]),
        pltpu.make_async_copy(x_hbm.at[:, CB - 1], held.at[0], sems.at[1]),
        pltpu.make_async_copy(x_hbm.at[:, 0], held.at[1], sems.at[2]),
    ]
    for copy in copies:
        copy.start()
    for copy in copies:
        copy.wait()
    for i, (out_ref, column) in enumerate(((to_right, CB - 1), (to_left, 0))):
        out_ref[...] = jnp.where(wet_ref[0, tile * blocks + column] > 0, held[i, 0], held[i, 1])


def early_kernel(levels, *refs):
    operands, send_in, mixed_ref, send_out = refs[:3], refs[3], refs[4], refs[5]
    send_out[...] = send_in[...]

    def run(*scratch):
        *loaded, sems = scratch
        copies = [
            pltpu.make_async_copy(a, b, sems.at[i]) for i, (a, b) in enumerate(zip(operands, loaded))
        ]
        for copy in copies:
            copy.start()
        for copy in copies:
            copy.wait()
        own_vertical(levels, *loaded, mixed_ref)

    @pl.when(lax.axis_index("tile") == 0)
    def _():
        pl.run_scoped(
            run,
            *[pltpu.VMEM(ref.shape, ref.dtype) for ref in operands],
            pltpu.SemaphoreType.DMA((len(operands),)),
        )


def vertical_kernel(levels, x_ref, w_vqkv, w_vout, early_ref, mixed_ref):
    @pl.when(lax.axis_index("tile") == 0)
    def _():
        mixed_ref[...] = early_ref[...]

    @pl.when(lax.axis_index("tile") != 0)
    def _():
        own_vertical(levels, x_ref, w_vqkv, w_vout, mixed_ref)


def own_vertical(levels, x_ref, w_vqkv, w_vout, mixed_ref):
    total_rows = x_ref.shape[0]
    group = min(max(levels, 128), total_rows)

    def mix(index):
        rows = rows_at(index * group, group)
        block = x_ref[rows, :]
        context = vertical_context(block, w_vqkv, levels)
        mixed_ref[rows, :] = (block.astype(F32) + dot(context, w_vout[...])).astype(BF)

    each(total_rows // group, mix)


def horizontal_kernel(
    levels, mixed_ref, wet_ref, w_hqkv, w_hout, result_ref, base_e, query_e, term_e, den_e
):
    total_rows, width = mixed_ref.shape
    size = width // HEADS
    blocks = total_rows // levels
    chunk = min(levels, 16)
    edges = [b for b in range(blocks) if b % CB in (0, CB - 1)]
    tile = lax.axis_index("tile")

    rows = blocks * chunk
    row = lax.broadcasted_iota(jnp.int32, (rows, rows), 0)
    col = lax.broadcasted_iota(jnp.int32, (rows, rows), 1)
    block_q, block_k = row // chunk, col // chunk
    wet = jnp.broadcast_to(wet_ref[...], (8, wet_ref.shape[1])).astype(BF)
    which = lax.broadcasted_iota(jnp.int32, (wet.shape[1], rows), 0)
    column = lax.broadcasted_iota(jnp.int32, (wet.shape[1], rows), 1) // chunk
    wet_k = dot(wet, (which == tile * blocks + column).astype(BF))[0:1, :]
    near = jnp.abs(block_q % CB - block_k % CB) <= 1
    near = near & (jnp.abs(block_q // CB - block_k // CB) <= 1)
    allowed = (row % chunk == col % chunk) & ((block_q == block_k) | (near & (wet_k > 0.5)))

    def attend(index):
        def spots(b):
            return rows_at(b * levels + index * chunk, chunk)

        mixed = jnp.concatenate([mixed_ref[spots(b), :] for b in range(blocks)], axis=0)
        values = mixed.astype(F32)
        joined = dot(rms_normed(values), w_hqkv[...])
        queries = normed_heads(joined[:, :width], size)
        keys = normed_heads(joined[:, width : 2 * width], size)
        parts, totals = attention(queries, keys, joined[:, 2 * width :].astype(BF), allowed)
        inner = [b for b in range(blocks) if b not in edges]

        def some(array, which):
            return jnp.concatenate([array[b * chunk : (b + 1) * chunk] for b in which], axis=0)

        context = jnp.concatenate([some(p, inner) for p in parts], axis=1)
        result = (some(values, inner) + dot(context, w_hout[...])).astype(BF)
        terms = [
            dot(some(p, edges), w_hout[h * size : (h + 1) * size, :]) for h, p in enumerate(parts)
        ]
        base = some(values, edges) + sum(terms)
        for i, b in enumerate(inner):
            result_ref[spots(b), :] = result[i * chunk : (i + 1) * chunk]
        for e, b in enumerate(edges):
            here = slice(e * chunk, (e + 1) * chunk)
            there = rows_at(e * levels + index * chunk, chunk)
            base_e[there, :] = base[here]
            for h in range(HEADS):
                cols = slice(h * size, (h + 1) * size)
                query_e[there, cols] = queries[h][b * chunk : (b + 1) * chunk].astype(F32)
                den_e[there, cols] = jnp.broadcast_to(
                    totals[h][b * chunk : (b + 1) * chunk], (chunk, size)
                )
                term_e[h, there, :] = terms[h][here]

    each(levels // chunk, attend)


def halo_kernel(
    levels, blocks, from_left, from_right, base_e, query_e, term_e, den_e,
    w_vqkv, w_vout, w_hqkv, w_hout, inner_ref, result_s,
):
    width = base_e.shape[1]
    size = width // HEADS
    scale = math.log2(math.e) / math.sqrt(size)
    chunk = min(levels, 16)
    edges = [b for b in range(blocks) if b % CB in (0, CB - 1)]
    group = 2 * levels if 2 * levels <= 128 else levels
    for b in range(blocks):
        if b not in edges:
            here = pl.ds(b * levels, levels)
            result_s[here, :] = inner_ref[here, :]

    halo = jnp.concatenate([from_left[...], from_right[...]], axis=0)
    heads = range(HEADS)
    pieces = []
    for start in range(0, 2 * levels, group):
        block = halo[start : start + group]
        context = halo_context(block, w_vqkv, levels)
        mixed = (block.astype(F32) + dot(context, w_vout[...])).astype(BF)
        joined = dot(mixed, w_hqkv[:, width:])
        mixed = mixed.astype(F32)
        squares = mean_square(mixed)
        values = (joined[:, width:] * lax.rsqrt(squares)).astype(BF)
        moved = []
        empty = jnp.zeros((group, size), BF)
        for h in range(0, HEADS, 2):
            one, two = head(values, h, size), head(values, h + 1, size)
            both = jnp.concatenate(
                [jnp.concatenate([one, empty], axis=1), jnp.concatenate([empty, two], axis=1)], axis=0
            )
            total = dot(both, w_hout[h * size : (h + 2) * size, :])
            moved += [total[:group], total[group:]]
        pieces.append((joined[:, :width], squares * EPSILON, *moved))
    keys, floor, *moved = (jnp.concatenate(p, axis=0) for p in zip(*pieces))

    for index in range(levels // chunk):
        def take(source, count):
            return jnp.concatenate(
                [source[i * levels + index * chunk :][:chunk] for i in range(count)], axis=0
            )

        def per_edge(values):
            sides = [values[:chunk], values[chunk:]]
            return jnp.concatenate([sides[0 if b % CB == 0 else 1] for b in edges], axis=0)

        def edge(*spot):
            return jnp.concatenate(
                [
                    ref[(*lead, pl.ds(e * levels + index * chunk, chunk), slice(None))]
                    for ref, *lead in [spot]
                    for e in range(len(edges))
                ],
                axis=0,
            )

        chunk_keys, chunk_floor = take(keys, 2), take(floor, 2)
        product = edge(query_e) * per_edge(chunk_keys)
        squares = chunk_keys * chunk_keys
        scores = [jnp.sum(head(product, h, size), axis=-1, keepdims=True) for h in heads]
        means = [jnp.mean(head(squares, h, size), axis=-1, keepdims=True) for h in heads]
        norms = [per_edge(lax.rsqrt(m + chunk_floor) * scale) for m in means]
        den = edge(den_e)
        shares = [
            1.0 / (1.0 + den[:, h * size : h * size + 1] * jnp.exp2(-(x * n)))
            for h, (x, n) in enumerate(zip(scores, norms))
        ]
        result = edge(base_e)
        for h, share in enumerate(shares):
            result = result + share * (per_edge(take(moved[h], 2)) - edge(term_e, h))
        result = result.astype(BF)
        for e, b in enumerate(edges):
            there = pl.ds(b * levels + index * chunk, chunk)
            result_s[there, :] = result[e * chunk : (e + 1) * chunk]


def on_device(state, wet, w_vqkv, w_vout, w_hqkv, w_hout):
    tiles = lax.axis_size("tile")
    blocks, levels, width = state.shape
    rows = blocks // CB
    edge_rows = 2 * rows * levels
    limit = (10 << 20) + levels * (256 << 10)
    vmem = pl.BlockSpec(memory_space=pltpu.VMEM)
    hbm = pl.BlockSpec(memory_space=pl.ANY)
    whole = jax.ShapeDtypeStruct((blocks * levels, width), BF)
    strip = state.reshape(rows, CB, levels, width)
    one = jax.ShapeDtypeStruct((levels, width), BF)
    to_right, to_left = pl.pallas_call(
        edge_kernel,
        out_shape=(one, one),
        in_specs=[hbm] * 2,
        out_specs=(vmem,) * 2,
        scratch_shapes=[
            pltpu.SMEM((1, wet.shape[0]), wet.dtype),
            pltpu.VMEM((2, rows, levels, width), BF),
            pltpu.SemaphoreType.DMA((3,)),
        ],
        compiler_params=pltpu.CompilerParams(vmem_limit_bytes=4 << 20),
        cost_estimate=pl.CostEstimate(flops=200 << 30, bytes_accessed=1 << 30, transcendentals=0),
        name="edge_blocks",
    )(*[pltpu.with_memory_space_constraint(v, pltpu.HBM) for v in (wet.reshape(1, -1), strip)])
    from_left = lax.ppermute(to_right, "tile", [(i, (i + 1) % tiles) for i in range(tiles)])
    edge_f32 = jax.ShapeDtypeStruct((edge_rows, width), F32)
    results = (
        whole,
        edge_f32,
        edge_f32,
        jax.ShapeDtypeStruct((HEADS, edge_rows, width), F32),
        edge_f32,
    )
    operands = (state.reshape(blocks * levels, width), w_vqkv, w_vout)
    work = blocks * levels * width * width
    cost = pl.CostEstimate(flops=8 * work, bytes_accessed=4 << 20, transcendentals=0)
    early, to_left = pl.pallas_call(
        functools.partial(early_kernel, levels),
        out_shape=(whole, one),
        in_specs=[hbm] * 3 + [vmem],
        out_specs=(vmem,) * 2,
        compiler_params=pltpu.CompilerParams(vmem_limit_bytes=limit),
        cost_estimate=cost,
        name="early_blocks",
    )(*[pltpu.with_memory_space_constraint(v, pltpu.HBM) for v in operands], to_left)
    from_right = lax.ppermute(to_left, "tile", [(i, (i - 1) % tiles) for i in range(tiles)])

    mixed = pl.pallas_call(
        functools.partial(vertical_kernel, levels),
        out_shape=whole,
        in_specs=[vmem] * 4,
        out_specs=vmem,
        compiler_params=pltpu.CompilerParams(vmem_limit_bytes=limit),
        cost_estimate=cost,
        name="vertical_blocks",
    )(*operands, early)
    inner, *edge_values = pl.pallas_call(
        functools.partial(horizontal_kernel, levels),
        out_shape=results,
        in_specs=[vmem] * 4,
        out_specs=(vmem,) * 5,
        compiler_params=pltpu.CompilerParams(vmem_limit_bytes=limit),
        cost_estimate=cost,
        name="horizontal_blocks",
    )(mixed, wet.reshape(1, -1), w_hqkv, w_hout)
    updated = pl.pallas_call(
        functools.partial(halo_kernel, levels, blocks),
        out_shape=whole,
        in_specs=[vmem] * 11,
        out_specs=vmem,
        compiler_params=pltpu.CompilerParams(vmem_limit_bytes=limit),
        name="halo_blocks",
    )(from_left, from_right, *edge_values, w_vqkv, w_vout, w_hqkv, w_hout, inner)
    return updated.reshape(blocks, levels, width)


def solution(mesh):
    in_specs = (P(("grp", "tile"), None, None), P(), P(), P(), P(), P())
    out_specs = P(("grp", "tile"), None, None)
    return jax.shard_map(
        on_device, mesh=mesh, in_specs=in_specs, out_specs=out_specs, check_vma=False
    )
```

```python
import functools
import math

import jax
import jax.numpy as jnp
from jax import lax
from jax.experimental import pallas as pl
from jax.experimental.pallas import tpu as pltpu
from jax.sharding import PartitionSpec as P

HEADS = 4
CB = 4
EPSILON = 1e-06
BF = jnp.bfloat16
F32 = jnp.float32


def each(count, body):
    if count == 1:
        body(0)
    else:
        pl.loop(0, count)(body)


def rows_at(start, size):
    if isinstance(start, int):
        return pl.ds(start, size)
    return pl.ds(pl.multiple_of(start, size), size)


def dot(left, right):
    return jnp.dot(left, right, preferred_element_type=F32)


def dot_t(left, right):
    return lax.dot_general(left, right, (((1,), (1,)), ((), ())), preferred_element_type=F32)


def head(values, index, size):
    return values[:, index * size : (index + 1) * size]


def with_ones(values):
    return jnp.concatenate([values, jnp.ones(values.shape, values.dtype)], axis=1)


def mean_square(values):
    return jnp.mean(values * values, axis=-1, keepdims=True) + EPSILON


def same_block(rows, levels):
    row = lax.broadcasted_iota(jnp.int32, (rows, rows), 0) // levels
    col = lax.broadcasted_iota(jnp.int32, (rows, rows), 1) // levels
    return row == col


def rms_normed(values):
    mean = jnp.mean(values * values, axis=-1, keepdims=True)
    return (values * lax.rsqrt(mean + EPSILON)).astype(BF)


def normed_heads(joined, size):
    return [rms_normed(head(joined, h, size)) for h in range(HEADS)]


def attention(queries, keys, values, allowed):
    size = queries[0].shape[1]
    scale = math.log2(math.e) / math.sqrt(size)
    scores = [dot_t(q, k) for q, k in zip(queries, keys)]
    expons = [jnp.exp2(x * scale) for x in scores]
    if allowed is not None:
        expons = [jnp.where(allowed, e, 0.0) for e in expons]
    totals = [jnp.sum(e, axis=-1, keepdims=True) for e in expons]
    probs = [(e / t).astype(BF) for e, t in zip(expons, totals)]
    contexts = [dot(p, head(values, h, size)).astype(BF) for h, p in enumerate(probs)]
    return contexts, totals


def vertical_context(block, w_vqkv, levels):
    rows, width = block.shape
    size = width // HEADS
    normed = rms_normed(block.astype(F32))
    keys = normed_heads(dot(normed, w_vqkv[:, width : 2 * width]), size)
    queries = normed_heads(dot(normed, w_vqkv[:, :width]), size)
    values = dot(normed, w_vqkv[:, 2 * width :]).astype(BF)
    allowed = same_block(rows, levels) if rows > levels else None
    return jnp.concatenate(attention(queries, keys, values, allowed)[0], axis=1)


def halo_context(block, w_vqkv, levels):
    rows, width = block.shape
    size = width // HEADS
    scale = math.log2(math.e) / math.sqrt(size)
    values = block.astype(F32)
    heads = range(HEADS)
    keys = dot(block, w_vqkv[:, width : 2 * width])
    queries = dot(block, w_vqkv[:, :width])
    vals = dot(block, w_vqkv[:, 2 * width :])
    squares = mean_square(values)
    squares_k = dot_t(jnp.full((8, width), 1.0 / width, BF), (values * values).astype(BF))[0:1]
    floor, floor_k = squares * EPSILON, (squares_k + EPSILON) * EPSILON
    keys_sq = (keys * keys).astype(BF)
    queries_b, keys_b = queries.astype(BF), keys.astype(BF)
    scores = [dot_t(head(queries_b, h, size), head(keys_b, h, size)) for h in heads]
    ones = jnp.full((8, size), 1.0 / size, BF)
    means_k = [dot_t(ones, head(keys_sq, h, size))[0:1] for h in heads]
    norms_q = [
        lax.rsqrt(jnp.mean(q * q, axis=-1, keepdims=True) + floor) * scale
        for q in (head(queries, h, size) for h in heads)
    ]
    norms_k = [lax.rsqrt(m + floor_k) for m in means_k]
    vals = (vals * lax.rsqrt(squares)).astype(BF)
    expons = [jnp.exp2(x * q * k) for x, q, k in zip(scores, norms_q, norms_k)]
    if rows > levels:
        inside = same_block(rows, levels)
        expons = [jnp.where(inside, e, 0.0) for e in expons]
    totals = [dot(e.astype(BF), with_ones(head(vals, h, size))) for h, e in enumerate(expons)]
    parts = [(t[:, :size] / t[:, size:]).astype(BF) for t in totals]
    return jnp.concatenate(parts, axis=1)


def edge_kernel(wet_hbm, x_hbm, to_right, to_left, wet_ref, held, sems):
    blocks = x_hbm.shape[0] * CB
    tile = lax.axis_index("tile")
    copies = [
        pltpu.make_async_copy(wet_hbm, wet_ref, sems.at[0]),
        pltpu.make_async_copy(x_hbm.at[:, CB - 1], held.at[0], sems.at[1]),
        pltpu.make_async_copy(x_hbm.at[:, 0], held.at[1], sems.at[2]),
    ]
    for copy in copies:
        copy.start()
    for copy in copies:
        copy.wait()
    for i, (out_ref, column) in enumerate(((to_right, CB - 1), (to_left, 0))):
        out_ref[...] = jnp.where(wet_ref[0, tile * blocks + column] > 0, held[i, 0], held[i, 1])


def early_kernel(levels, *refs):
    operands, send_in, mixed_ref, send_out = refs[:3], refs[3], refs[4], refs[5]
    send_out[...] = send_in[...]

    def run(*scratch):
        *loaded, sems = scratch
        copies = [
            pltpu.make_async_copy(a, b, sems.at[i]) for i, (a, b) in enumerate(zip(operands, loaded))
        ]
        for copy in copies:
            copy.start()
        for copy in copies:
            copy.wait()
        own_vertical(levels, *loaded, mixed_ref)

    @pl.when(lax.axis_index("tile") == 0)
    def _():
        pl.run_scoped(
            run,
            *[pltpu.VMEM(ref.shape, ref.dtype) for ref in operands],
            pltpu.SemaphoreType.DMA((len(operands),)),
        )


def vertical_kernel(levels, x_ref, w_vqkv, w_vout, early_ref, mixed_ref):
    @pl.when(lax.axis_index("tile") == 0)
    def _():
        mixed_ref[...] = early_ref[...]

    @pl.when(lax.axis_index("tile") != 0)
    def _():
        own_vertical(levels, x_ref, w_vqkv, w_vout, mixed_ref)


def own_vertical(levels, x_ref, w_vqkv, w_vout, mixed_ref):
    total_rows = x_ref.shape[0]
    group = min(max(levels, 128), total_rows)

    def mix(index):
        rows = rows_at(index * group, group)
        block = x_ref[rows, :]
        context = vertical_context(block, w_vqkv, levels)
        mixed_ref[rows, :] = (block.astype(F32) + dot(context, w_vout[...])).astype(BF)

    each(total_rows // group, mix)


def horizontal_kernel(
    levels, mixed_ref, wet_ref, w_hqkv, w_hout, result_ref, base_e, query_e, term_e, den_e
):
    total_rows, width = mixed_ref.shape
    size = width // HEADS
    blocks = total_rows // levels
    chunk = min(levels, 16)
    edges = [b for b in range(blocks) if b % CB in (0, CB - 1)]
    tile = lax.axis_index("tile")

    rows = blocks * chunk
    row = lax.broadcasted_iota(jnp.int32, (rows, rows), 0)
    col = lax.broadcasted_iota(jnp.int32, (rows, rows), 1)
    block_q, block_k = row // chunk, col // chunk
    wet = jnp.broadcast_to(wet_ref[...], (8, wet_ref.shape[1])).astype(BF)
    which = lax.broadcasted_iota(jnp.int32, (wet.shape[1], rows), 0)
    column = lax.broadcasted_iota(jnp.int32, (wet.shape[1], rows), 1) // chunk
    wet_k = dot(wet, (which == tile * blocks + column).astype(BF))[0:1, :]
    near = jnp.abs(block_q % CB - block_k % CB) <= 1
    near = near & (jnp.abs(block_q // CB - block_k // CB) <= 1)
    allowed = (row % chunk == col % chunk) & ((block_q == block_k) | (near & (wet_k > 0.5)))

    def attend(index):
        def spots(b):
            return rows_at(b * levels + index * chunk, chunk)

        mixed = jnp.concatenate([mixed_ref[spots(b), :] for b in range(blocks)], axis=0)
        values = mixed.astype(F32)
        joined = dot(rms_normed(values), w_hqkv[...])
        queries = normed_heads(joined[:, :width], size)
        keys = normed_heads(joined[:, width : 2 * width], size)
        parts, totals = attention(queries, keys, joined[:, 2 * width :].astype(BF), allowed)
        inner = [b for b in range(blocks) if b not in edges]

        def some(array, which):
            return jnp.concatenate([array[b * chunk : (b + 1) * chunk] for b in which], axis=0)

        context = jnp.concatenate([some(p, inner) for p in parts], axis=1)
        result = (some(values, inner) + dot(context, w_hout[...])).astype(BF)
        terms = [
            dot(some(p, edges), w_hout[h * size : (h + 1) * size, :]) for h, p in enumerate(parts)
        ]
        base = some(values, edges) + sum(terms)
        for i, b in enumerate(inner):
            result_ref[spots(b), :] = result[i * chunk : (i + 1) * chunk]
        for e, b in enumerate(edges):
            here = slice(e * chunk, (e + 1) * chunk)
            there = rows_at(e * levels + index * chunk, chunk)
            base_e[there, :] = base[here]
            for h in range(HEADS):
                cols = slice(h * size, (h + 1) * size)
                query_e[there, cols] = queries[h][b * chunk : (b + 1) * chunk].astype(F32)
                den_e[there, cols] = jnp.broadcast_to(
                    totals[h][b * chunk : (b + 1) * chunk], (chunk, size)
                )
                term_e[h, there, :] = terms[h][here]

    each(levels // chunk, attend)


def halo_kernel(
    levels, blocks, from_left, from_right, base_e, query_e, term_e, den_e,
    w_vqkv, w_vout, w_hqkv, w_hout, inner_ref, result_s,
):
    width = base_e.shape[1]
    size = width // HEADS
    scale = math.log2(math.e) / math.sqrt(size)
    chunk = min(levels, 16)
    edges = [b for b in range(blocks) if b % CB in (0, CB - 1)]
    group = 2 * levels if 2 * levels <= 128 else levels
    for b in range(blocks):
        if b not in edges:
            here = pl.ds(b * levels, levels)
            result_s[here, :] = inner_ref[here, :]

    halo = jnp.concatenate([from_left[...], from_right[...]], axis=0)
    heads = range(HEADS)
    pieces = []
    for start in range(0, 2 * levels, group):
        block = halo[start : start + group]
        context = halo_context(block, w_vqkv, levels)
        mixed = (block.astype(F32) + dot(context, w_vout[...])).astype(BF)
        joined = dot(mixed, w_hqkv[:, width:])
        mixed = mixed.astype(F32)
        squares = mean_square(mixed)
        values = (joined[:, width:] * lax.rsqrt(squares)).astype(BF)
        moved = []
        empty = jnp.zeros((group, size), BF)
        for h in range(0, HEADS, 2):
            one, two = head(values, h, size), head(values, h + 1, size)
            both = jnp.concatenate(
                [jnp.concatenate([one, empty], axis=1), jnp.concatenate([empty, two], axis=1)], axis=0
            )
            total = dot(both, w_hout[h * size : (h + 2) * size, :])
            moved += [total[:group], total[group:]]
        pieces.append((joined[:, :width], squares * EPSILON, *moved))
    keys, floor, *moved = (jnp.concatenate(p, axis=0) for p in zip(*pieces))

    for index in range(levels // chunk):
        def take(source, count):
            return jnp.concatenate(
                [source[i * levels + index * chunk :][:chunk] for i in range(count)], axis=0
            )

        def per_edge(values):
            sides = [values[:chunk], values[chunk:]]
            return jnp.concatenate([sides[0 if b % CB == 0 else 1] for b in edges], axis=0)

        def edge(*spot):
            return jnp.concatenate(
                [
                    ref[(*lead, pl.ds(e * levels + index * chunk, chunk), slice(None))]
                    for ref, *lead in [spot]
                    for e in range(len(edges))
                ],
                axis=0,
            )

        chunk_keys, chunk_floor = take(keys, 2), take(floor, 2)
        product = edge(query_e) * per_edge(chunk_keys)
        squares = chunk_keys * chunk_keys
        scores = [jnp.sum(head(product, h, size), axis=-1, keepdims=True) for h in heads]
        means = [jnp.mean(head(squares, h, size), axis=-1, keepdims=True) for h in heads]
        norms = [per_edge(lax.rsqrt(m + chunk_floor) * scale) for m in means]
        den = edge(den_e)
        shares = [
            1.0 / (1.0 + den[:, h * size : h * size + 1] * jnp.exp2(-(x * n)))
            for h, (x, n) in enumerate(zip(scores, norms))
        ]
        result = edge(base_e)
        for h, share in enumerate(shares):
            result = result + share * (per_edge(take(moved[h], 2)) - edge(term_e, h))
        result = result.astype(BF)
        for e, b in enumerate(edges):
            there = pl.ds(b * levels + index * chunk, chunk)
            result_s[there, :] = result[e * chunk : (e + 1) * chunk]


def on_device(state, wet, w_vqkv, w_vout, w_hqkv, w_hout):
    tiles = lax.axis_size("tile")
    blocks, levels, width = state.shape
    rows = blocks // CB
    edge_rows = 2 * rows * levels
    limit = (10 << 20) + levels * (256 << 10)
    vmem = pl.BlockSpec(memory_space=pltpu.VMEM)
    hbm = pl.BlockSpec(memory_space=pl.ANY)
    whole = jax.ShapeDtypeStruct((blocks * levels, width), BF)
    strip = state.reshape(rows, CB, levels, width)
    one = jax.ShapeDtypeStruct((levels, width), BF)
    to_right, to_left = pl.pallas_call(
        edge_kernel,
        out_shape=(one, one),
        in_specs=[hbm] * 2,
        out_specs=(vmem,) * 2,
        scratch_shapes=[
            pltpu.SMEM((1, wet.shape[0]), wet.dtype),
            pltpu.VMEM((2, rows, levels, width), BF),
            pltpu.SemaphoreType.DMA((3,)),
        ],
        compiler_params=pltpu.CompilerParams(vmem_limit_bytes=4 << 20),
        cost_estimate=pl.CostEstimate(flops=200 << 30, bytes_accessed=1 << 30, transcendentals=0),
        name="edge_blocks",
    )(*[pltpu.with_memory_space_constraint(v, pltpu.HBM) for v in (wet.reshape(1, -1), strip)])
    from_left = lax.ppermute(to_right, "tile", [(i, (i + 1) % tiles) for i in range(tiles)])
    edge_f32 = jax.ShapeDtypeStruct((edge_rows, width), F32)
    results = (
        whole,
        edge_f32,
        edge_f32,
        jax.ShapeDtypeStruct((HEADS, edge_rows, width), F32),
        edge_f32,
    )
    operands = (state.reshape(blocks * levels, width), w_vqkv, w_vout)
    work = blocks * levels * width * width
    cost = pl.CostEstimate(flops=8 * work, bytes_accessed=4 << 20, transcendentals=0)
    early, to_left = pl.pallas_call(
        functools.partial(early_kernel, levels),
        out_shape=(whole, one),
        in_specs=[hbm] * 3 + [vmem],
        out_specs=(vmem,) * 2,
        compiler_params=pltpu.CompilerParams(vmem_limit_bytes=limit),
        cost_estimate=pl.CostEstimate(flops=64 * work, bytes_accessed=16 << 20, transcendentals=0),
        name="early_blocks",
    )(*[pltpu.with_memory_space_constraint(v, pltpu.HBM) for v in operands], to_left)
    from_right = lax.ppermute(to_left, "tile", [(i, (i - 1) % tiles) for i in range(tiles)])

    mixed = pl.pallas_call(
        functools.partial(vertical_kernel, levels),
        out_shape=whole,
        in_specs=[vmem] * 4,
        out_specs=vmem,
        compiler_params=pltpu.CompilerParams(vmem_limit_bytes=limit),
        cost_estimate=cost,
        name="vertical_blocks",
    )(*operands, early)
    inner, *edge_values = pl.pallas_call(
        functools.partial(horizontal_kernel, levels),
        out_shape=results,
        in_specs=[vmem] * 4,
        out_specs=(vmem,) * 5,
        compiler_params=pltpu.CompilerParams(vmem_limit_bytes=limit),
        cost_estimate=cost,
        name="horizontal_blocks",
    )(mixed, wet.reshape(1, -1), w_hqkv, w_hout)
    updated = pl.pallas_call(
        functools.partial(halo_kernel, levels, blocks),
        out_shape=whole,
        in_specs=[vmem] * 11,
        out_specs=vmem,
        compiler_params=pltpu.CompilerParams(vmem_limit_bytes=limit),
        name="halo_blocks",
    )(from_left, from_right, *edge_values, w_vqkv, w_vout, w_hqkv, w_hout, inner)
    return updated.reshape(blocks, levels, width)


def solution(mesh):
    in_specs = (P(("grp", "tile"), None, None), P(), P(), P(), P(), P())
    out_specs = P(("grp", "tile"), None, None)
    return jax.shard_map(
        on_device, mesh=mesh, in_specs=in_specs, out_specs=out_specs, check_vma=False
    )
```

```python
import functools
import math

import jax
import jax.numpy as jnp
from jax import lax
from jax.experimental import pallas as pl
from jax.experimental.pallas import tpu as pltpu
from jax.sharding import PartitionSpec as P

HEADS = 4
CB = 4
EPSILON = 1e-06
BF = jnp.bfloat16
F32 = jnp.float32


def each(count, body):
    if count == 1:
        body(0)
    else:
        pl.loop(0, count)(body)


def rows_at(start, size):
    if isinstance(start, int):
        return pl.ds(start, size)
    return pl.ds(pl.multiple_of(start, size), size)


def dot(left, right):
    return jnp.dot(left, right, preferred_element_type=F32)


def dot_t(left, right):
    return lax.dot_general(left, right, (((1,), (1,)), ((), ())), preferred_element_type=F32)


def head(values, index, size):
    return values[:, index * size : (index + 1) * size]


def with_ones(values):
    return jnp.concatenate([values, jnp.ones(values.shape, values.dtype)], axis=1)


def mean_square(values):
    return jnp.mean(values * values, axis=-1, keepdims=True) + EPSILON


def same_block(rows, levels):
    row = lax.broadcasted_iota(jnp.int32, (rows, rows), 0) // levels
    col = lax.broadcasted_iota(jnp.int32, (rows, rows), 1) // levels
    return row == col


def rms_normed(values):
    mean = jnp.mean(values * values, axis=-1, keepdims=True)
    return (values * lax.rsqrt(mean + EPSILON)).astype(BF)


def normed_heads(joined, size):
    return [rms_normed(head(joined, h, size)) for h in range(HEADS)]


def attention(queries, keys, values, allowed):
    size = queries[0].shape[1]
    scale = math.log2(math.e) / math.sqrt(size)
    scores = [dot_t(q, k) for q, k in zip(queries, keys)]
    expons = [jnp.exp2(x * scale) for x in scores]
    if allowed is not None:
        expons = [jnp.where(allowed, e, 0.0) for e in expons]
    totals = [jnp.sum(e, axis=-1, keepdims=True) for e in expons]
    probs = [(e / t).astype(BF) for e, t in zip(expons, totals)]
    contexts = [dot(p, head(values, h, size)).astype(BF) for h, p in enumerate(probs)]
    return contexts, totals


def vertical_context(block, w_vqkv, levels):
    rows, width = block.shape
    size = width // HEADS
    normed = rms_normed(block.astype(F32))
    keys = normed_heads(dot(normed, w_vqkv[:, width : 2 * width]), size)
    queries = normed_heads(dot(normed, w_vqkv[:, :width]), size)
    values = dot(normed, w_vqkv[:, 2 * width :]).astype(BF)
    allowed = same_block(rows, levels) if rows > levels else None
    return jnp.concatenate(attention(queries, keys, values, allowed)[0], axis=1)


def halo_context(block, w_vqkv, levels):
    rows, width = block.shape
    size = width // HEADS
    scale = math.log2(math.e) / math.sqrt(size)
    values = block.astype(F32)
    heads = range(HEADS)
    keys = dot(block, w_vqkv[:, width : 2 * width])
    queries = dot(block, w_vqkv[:, :width])
    vals = dot(block, w_vqkv[:, 2 * width :])
    squares = mean_square(values)
    squares_k = dot_t(jnp.full((8, width), 1.0 / width, BF), (values * values).astype(BF))[0:1]
    floor, floor_k = squares * EPSILON, (squares_k + EPSILON) * EPSILON
    keys_sq = (keys * keys).astype(BF)
    queries_b, keys_b = queries.astype(BF), keys.astype(BF)
    scores = [dot_t(head(queries_b, h, size), head(keys_b, h, size)) for h in heads]
    ones = jnp.full((8, size), 1.0 / size, BF)
    means_k = [dot_t(ones, head(keys_sq, h, size))[0:1] for h in heads]
    norms_q = [
        lax.rsqrt(jnp.mean(q * q, axis=-1, keepdims=True) + floor) * scale
        for q in (head(queries, h, size) for h in heads)
    ]
    norms_k = [lax.rsqrt(m + floor_k) for m in means_k]
    vals = (vals * lax.rsqrt(squares)).astype(BF)
    expons = [jnp.exp2(x * q * k) for x, q, k in zip(scores, norms_q, norms_k)]
    if rows > levels:
        inside = same_block(rows, levels)
        expons = [jnp.where(inside, e, 0.0) for e in expons]
    totals = [dot(e.astype(BF), with_ones(head(vals, h, size))) for h, e in enumerate(expons)]
    parts = [(t[:, :size] / t[:, size:]).astype(BF) for t in totals]
    return jnp.concatenate(parts, axis=1)


def edge_kernel(wet_hbm, x_hbm, to_right, to_left, wet_ref, held, sems):
    blocks = x_hbm.shape[0] * CB
    tile = lax.axis_index("tile")
    copies = [
        pltpu.make_async_copy(wet_hbm, wet_ref, sems.at[0]),
        pltpu.make_async_copy(x_hbm.at[:, CB - 1], held.at[0], sems.at[1]),
        pltpu.make_async_copy(x_hbm.at[:, 0], held.at[1], sems.at[2]),
    ]
    for copy in copies:
        copy.start()
    for copy in copies:
        copy.wait()
    for i, (out_ref, column) in enumerate(((to_right, CB - 1), (to_left, 0))):
        out_ref[...] = jnp.where(wet_ref[0, tile * blocks + column] > 0, held[i, 0], held[i, 1])


def early_kernel(levels, *refs):
    operands, send_in, mixed_ref, send_out = refs[:3], refs[3], refs[4], refs[5]
    send_out[...] = send_in[...]

    def run(*scratch):
        *loaded, sems = scratch
        copies = [
            pltpu.make_async_copy(a, b, sems.at[i]) for i, (a, b) in enumerate(zip(operands, loaded))
        ]
        for copy in copies:
            copy.start()
        for copy in copies:
            copy.wait()
        own_vertical(levels, *loaded, mixed_ref)

    @pl.when(lax.axis_index("tile") == 0)
    def _():
        pl.run_scoped(
            run,
            *[pltpu.VMEM(ref.shape, ref.dtype) for ref in operands],
            pltpu.SemaphoreType.DMA((len(operands),)),
        )


def vertical_kernel(levels, x_ref, w_vqkv, w_vout, early_ref, mixed_ref):
    @pl.when(lax.axis_index("tile") == 0)
    def _():
        mixed_ref[...] = early_ref[...]

    @pl.when(lax.axis_index("tile") != 0)
    def _():
        own_vertical(levels, x_ref, w_vqkv, w_vout, mixed_ref)


def own_vertical(levels, x_ref, w_vqkv, w_vout, mixed_ref):
    total_rows = x_ref.shape[0]
    group = min(max(levels, 128), total_rows)

    def mix(index):
        rows = rows_at(index * group, group)
        block = x_ref[rows, :]
        context = vertical_context(block, w_vqkv, levels)
        mixed_ref[rows, :] = (block.astype(F32) + dot(context, w_vout[...])).astype(BF)

    each(total_rows // group, mix)


def horizontal_kernel(
    levels, mixed_ref, wet_ref, w_hqkv, w_hout, result_ref, base_e, query_e, term_e, den_e
):
    total_rows, width = mixed_ref.shape
    size = width // HEADS
    blocks = total_rows // levels
    chunk = min(levels, 16)
    edges = [b for b in range(blocks) if b % CB in (0, CB - 1)]
    tile = lax.axis_index("tile")

    rows = blocks * chunk
    row = lax.broadcasted_iota(jnp.int32, (rows, rows), 0)
    col = lax.broadcasted_iota(jnp.int32, (rows, rows), 1)
    block_q, block_k = row // chunk, col // chunk
    wet = jnp.broadcast_to(wet_ref[...], (8, wet_ref.shape[1])).astype(BF)
    which = lax.broadcasted_iota(jnp.int32, (wet.shape[1], rows), 0)
    column = lax.broadcasted_iota(jnp.int32, (wet.shape[1], rows), 1) // chunk
    wet_k = dot(wet, (which == tile * blocks + column).astype(BF))[0:1, :]
    near = jnp.abs(block_q % CB - block_k % CB) <= 1
    near = near & (jnp.abs(block_q // CB - block_k // CB) <= 1)
    allowed = (row % chunk == col % chunk) & ((block_q == block_k) | (near & (wet_k > 0.5)))

    def attend(index):
        def spots(b):
            return rows_at(b * levels + index * chunk, chunk)

        mixed = jnp.concatenate([mixed_ref[spots(b), :] for b in range(blocks)], axis=0)
        values = mixed.astype(F32)
        joined = dot(rms_normed(values), w_hqkv[...])
        queries = normed_heads(joined[:, :width], size)
        keys = normed_heads(joined[:, width : 2 * width], size)
        parts, totals = attention(queries, keys, joined[:, 2 * width :].astype(BF), allowed)
        inner = [b for b in range(blocks) if b not in edges]

        def some(array, which):
            return jnp.concatenate([array[b * chunk : (b + 1) * chunk] for b in which], axis=0)

        context = jnp.concatenate([some(p, inner) for p in parts], axis=1)
        result = (some(values, inner) + dot(context, w_hout[...])).astype(BF)
        terms = [
            dot(some(p, edges), w_hout[h * size : (h + 1) * size, :]) for h, p in enumerate(parts)
        ]
        base = some(values, edges) + sum(terms)
        for i, b in enumerate(inner):
            result_ref[spots(b), :] = result[i * chunk : (i + 1) * chunk]
        for e, b in enumerate(edges):
            here = slice(e * chunk, (e + 1) * chunk)
            there = rows_at(e * levels + index * chunk, chunk)
            base_e[there, :] = base[here]
            for h in range(HEADS):
                cols = slice(h * size, (h + 1) * size)
                query_e[there, cols] = queries[h][b * chunk : (b + 1) * chunk].astype(F32)
                den_e[there, cols] = jnp.broadcast_to(
                    totals[h][b * chunk : (b + 1) * chunk], (chunk, size)
                )
                term_e[h, there, :] = terms[h][here].astype(BF)

    each(levels // chunk, attend)


def halo_kernel(
    levels, blocks, from_left, from_right, base_e, query_e, term_e, den_e,
    w_vqkv, w_vout, w_hqkv, w_hout, inner_ref, result_s,
):
    width = base_e.shape[1]
    size = width // HEADS
    scale = math.log2(math.e) / math.sqrt(size)
    chunk = min(levels, 16)
    edges = [b for b in range(blocks) if b % CB in (0, CB - 1)]
    group = 2 * levels if 2 * levels <= 128 else levels
    for b in range(blocks):
        if b not in edges:
            here = pl.ds(b * levels, levels)
            result_s[here, :] = inner_ref[here, :]

    halo = jnp.concatenate([from_left[...], from_right[...]], axis=0)
    heads = range(HEADS)
    pieces = []
    for start in range(0, 2 * levels, group):
        block = halo[start : start + group]
        context = halo_context(block, w_vqkv, levels)
        mixed = (block.astype(F32) + dot(context, w_vout[...])).astype(BF)
        joined = dot(mixed, w_hqkv[:, width:])
        mixed = mixed.astype(F32)
        squares = mean_square(mixed)
        values = (joined[:, width:] * lax.rsqrt(squares)).astype(BF)
        moved = []
        empty = jnp.zeros((group, size), BF)
        for h in range(0, HEADS, 2):
            one, two = head(values, h, size), head(values, h + 1, size)
            both = jnp.concatenate(
                [jnp.concatenate([one, empty], axis=1), jnp.concatenate([empty, two], axis=1)], axis=0
            )
            total = dot(both, w_hout[h * size : (h + 2) * size, :])
            moved += [total[:group], total[group:]]
        pieces.append((joined[:, :width], squares * EPSILON, *moved))
    keys, floor, *moved = (jnp.concatenate(p, axis=0) for p in zip(*pieces))

    for index in range(levels // chunk):
        def take(source, count):
            return jnp.concatenate(
                [source[i * levels + index * chunk :][:chunk] for i in range(count)], axis=0
            )

        def per_edge(values):
            sides = [values[:chunk], values[chunk:]]
            return jnp.concatenate([sides[0 if b % CB == 0 else 1] for b in edges], axis=0)

        def edge(*spot):
            return jnp.concatenate(
                [
                    ref[(*lead, pl.ds(e * levels + index * chunk, chunk), slice(None))]
                    for ref, *lead in [spot]
                    for e in range(len(edges))
                ],
                axis=0,
            )

        chunk_keys, chunk_floor = take(keys, 2), take(floor, 2)
        product = edge(query_e) * per_edge(chunk_keys)
        squares = chunk_keys * chunk_keys
        scores = [jnp.sum(head(product, h, size), axis=-1, keepdims=True) for h in heads]
        means = [jnp.mean(head(squares, h, size), axis=-1, keepdims=True) for h in heads]
        norms = [per_edge(lax.rsqrt(m + chunk_floor) * scale) for m in means]
        den = edge(den_e)
        shares = [
            1.0 / (1.0 + den[:, h * size : h * size + 1] * jnp.exp2(-(x * n)))
            for h, (x, n) in enumerate(zip(scores, norms))
        ]
        result = edge(base_e)
        for h, share in enumerate(shares):
            result = result + share * (per_edge(take(moved[h], 2)) - edge(term_e, h).astype(F32))
        result = result.astype(BF)
        for e, b in enumerate(edges):
            there = pl.ds(b * levels + index * chunk, chunk)
            result_s[there, :] = result[e * chunk : (e + 1) * chunk]


def on_device(state, wet, w_vqkv, w_vout, w_hqkv, w_hout):
    tiles = lax.axis_size("tile")
    blocks, levels, width = state.shape
    rows = blocks // CB
    edge_rows = 2 * rows * levels
    limit = (10 << 20) + levels * (256 << 10)
    vmem = pl.BlockSpec(memory_space=pltpu.VMEM)
    hbm = pl.BlockSpec(memory_space=pl.ANY)
    whole = jax.ShapeDtypeStruct((blocks * levels, width), BF)
    strip = state.reshape(rows, CB, levels, width)
    one = jax.ShapeDtypeStruct((levels, width), BF)
    to_right, to_left = pl.pallas_call(
        edge_kernel,
        out_shape=(one, one),
        in_specs=[hbm] * 2,
        out_specs=(vmem,) * 2,
        scratch_shapes=[
            pltpu.SMEM((1, wet.shape[0]), wet.dtype),
            pltpu.VMEM((2, rows, levels, width), BF),
            pltpu.SemaphoreType.DMA((3,)),
        ],
        compiler_params=pltpu.CompilerParams(vmem_limit_bytes=4 << 20),
        cost_estimate=pl.CostEstimate(flops=200 << 30, bytes_accessed=1 << 30, transcendentals=0),
        name="edge_blocks",
    )(*[pltpu.with_memory_space_constraint(v, pltpu.HBM) for v in (wet.reshape(1, -1), strip)])
    from_left = lax.ppermute(to_right, "tile", [(i, (i + 1) % tiles) for i in range(tiles)])
    edge_f32 = jax.ShapeDtypeStruct((edge_rows, width), F32)
    results = (
        whole,
        edge_f32,
        edge_f32,
        jax.ShapeDtypeStruct((HEADS, edge_rows, width), BF),
        edge_f32,
    )
    operands = (state.reshape(blocks * levels, width), w_vqkv, w_vout)
    work = blocks * levels * width * width
    cost = pl.CostEstimate(flops=8 * work, bytes_accessed=4 << 20, transcendentals=0)
    early, to_left = pl.pallas_call(
        functools.partial(early_kernel, levels),
        out_shape=(whole, one),
        in_specs=[hbm] * 3 + [vmem],
        out_specs=(vmem,) * 2,
        compiler_params=pltpu.CompilerParams(vmem_limit_bytes=limit),
        cost_estimate=cost,
        name="early_blocks",
    )(*[pltpu.with_memory_space_constraint(v, pltpu.HBM) for v in operands], to_left)
    from_right = lax.ppermute(to_left, "tile", [(i, (i - 1) % tiles) for i in range(tiles)])

    mixed = pl.pallas_call(
        functools.partial(vertical_kernel, levels),
        out_shape=whole,
        in_specs=[vmem] * 4,
        out_specs=vmem,
        compiler_params=pltpu.CompilerParams(vmem_limit_bytes=limit),
        cost_estimate=cost,
        name="vertical_blocks",
    )(*operands, early)
    inner, *edge_values = pl.pallas_call(
        functools.partial(horizontal_kernel, levels),
        out_shape=results,
        in_specs=[vmem] * 4,
        out_specs=(vmem,) * 5,
        compiler_params=pltpu.CompilerParams(vmem_limit_bytes=limit),
        cost_estimate=cost,
        name="horizontal_blocks",
    )(mixed, wet.reshape(1, -1), w_hqkv, w_hout)
    updated = pl.pallas_call(
        functools.partial(halo_kernel, levels, blocks),
        out_shape=whole,
        in_specs=[vmem] * 11,
        out_specs=vmem,
        compiler_params=pltpu.CompilerParams(vmem_limit_bytes=limit),
        name="halo_blocks",
    )(from_left, from_right, *edge_values, w_vqkv, w_vout, w_hqkv, w_hout, inner)
    return updated.reshape(blocks, levels, width)


def solution(mesh):
    in_specs = (P(("grp", "tile"), None, None), P(), P(), P(), P(), P())
    out_specs = P(("grp", "tile"), None, None)
    return jax.shard_map(
        on_device, mesh=mesh, in_specs=in_specs, out_specs=out_specs, check_vma=False
    )
```
